32 devices in a mesh: hst: 4 (over y, x), dev: 8 (over z, core).
Axes of the slice: x: 2, y: 2, z: 4, core: 2. Of those that a mesh axis runs over, the one named last changes fastest.
Arguments:
- replay: bfloat16 [4096, 28224], P(('hst', 'dev')), may hold values from 0 to 1
- send_index: int32 [32, 32, 8], P(('hst', 'dev')), may hold values from 0 to 127
- send_count: int32 [32, 32], P(('hst', 'dev')), may hold values from 0 to 8, as said below
- actions: int32 [32, 32, 8], P(('hst', 'dev')), may hold values from 0 to 17
- game_ids: int32 [32, 32, 8], P(('hst', 'dev')), may hold values from 0 to 56
- legal_table: int32 [57, 18], replicated, may hold values 0 or 1
- returns: float32 [32, 32, 8], P(('hst', 'dev')), may hold values from -6 to 6
- bootstrap: float32 [32, 32, 8], P(('hst', 'dev')), may hold values from -6 to 6
- is_weights: float32 [32, 32, 8], P(('hst', 'dev')), may hold values from 0.1 to 1
- priority_table: float32 [4096], P(('hst', 'dev')), may hold values from 0.3 to 3
- conv1_w: bfloat16 [8, 8, 4, 32], replicated, may hold values from -0.375 to 0.375
- conv1_b: bfloat16 [32], replicated, may hold values from -1.5 to 1.5
- conv2_w: bfloat16 [4, 4, 32, 64], replicated, may hold values from -0.25 to 0.25
- conv2_b: bfloat16 [64], replicated, may hold values from -1.5 to 1.5
- conv3_w: bfloat16 [3, 3, 64, 64], replicated, may hold values from -0.25 to 0.25
- conv3_b: bfloat16 [64], replicated, may hold values from -1.5 to 1.5
- dense_w: bfloat16 [3136, 512], replicated, may hold values from -0.109375 to 0.109375
- dense_b: bfloat16 [512], replicated, may hold values from -1.5 to 1.5
- value_w: bfloat16 [512, 1], replicated, may hold values from -0.25 to 0.25
- value_b: bfloat16 [1], replicated, may hold values from -1.5 to 1.5
- advantage_w: bfloat16 [512, 18], replicated, may hold values from -0.25 to 0.25
- advantage_b: bfloat16 [18], replicated, may hold values from -1.5 to 1.5
Outputs:
- q_values: float32 [32, 256, 18], P(('hst', 'dev'))
- loss: float32 [], replicated
- grad_conv1_w: float32 [8, 8, 4, 32], replicated
- grad_conv1_b: float32 [32], replicated
- grad_conv2_w: float32 [4, 4, 32, 64], replicated
- grad_conv2_b: float32 [64], replicated
- grad_conv3_w: float32 [3, 3, 64, 64], replicated
- grad_conv3_b: float32 [64], replicated
- grad_dense_w: float32 [3136, 512], replicated
- grad_dense_b: float32 [512], replicated
- grad_value_w: float32 [512, 1], replicated
- grad_value_b: float32 [1], replicated
- grad_advantage_w: float32 [512, 18], replicated
- grad_advantage_b: float32 [18], replicated
- new_table: float32 [4096], P(('hst', 'dev'))
- top_priority: float32 [], replicated
The draws below stay inside these ranges and needn't reach their ends.
Inputs may be any that keep to these rules, and one draw needn't show every extreme that they name: `send_count`: in every draw one learner receives 8 live slots from every owner.
All inputs are finite; a program needn't handle non-finite values.
Results may differ from the reference program's by a relative error of at most 0.0021.
Values may be sent and summed in bfloat16 or wider, within the bound.
A program may use at most 192 MiB of HBM per device.

```python
import math
import jax
import jax.numpy as jnp
from jax import lax

FRAME = 84
STACK = 4
C1 = 32
C2 = 64
C3 = 64
HIDDEN_SIZE = 512
ACTIONS = 18
GAMES = 57
K1 = 8
S1 = 4
K2 = 4
S2 = 2
K3 = 3
S3 = 1
FLAT = 3136
SLOTS_DEV = 256
CAP = 8
R_DEV = 128
R_TOTAL = 4096
DEVICES = 32


def draw_send_count(key, part):
    key = jax.random.fold_in(key, 11)
    heat_key, raw_key, full_key = jax.random.split(key, 3)
    heat = jax.random.randint(heat_key, (DEVICES, 1), 1, 5)
    raw_count = jax.random.randint(raw_key, (DEVICES, DEVICES), 0, CAP + 1)
    counted = jnp.minimum(CAP, raw_count * heat // 2)
    full_column = jax.random.randint(full_key, (), 0, DEVICES)
    counted = jnp.where(jnp.arange(DEVICES)[None, :] == full_column, CAP, counted)
    return counted.astype(jnp.int32)


def draw_priority_table(key, part):
    key = jax.random.fold_in(key, 23)
    owner_rank = (jnp.arange(R_TOTAL) // R_DEV).astype(jnp.float32)
    rising = 1.0 + 2.0 * owner_rank / max(R_TOTAL // R_DEV - 1, 1)
    spread = jax.random.uniform(key, (R_TOTAL,), jnp.float32, jnp.log(0.3), 0.0)
    return (jnp.exp(spread) * rising).astype(jnp.float32)


def touch_ends(entries, key, smallest, high):
    dims = entries.shape
    place = [jax.random.randint(jax.random.fold_in(key, axis), (), 0, dims[axis]) for axis in range(len(dims))]
    entries = entries.at[tuple(place)].set(smallest)
    longest = dims.index(max(dims))
    place[longest] = (place[longest] + 1) % dims[longest]
    return entries.at[tuple(place)].set(high)


def level_of(own_key, shape, cuts, smallest, high):
    factor_of = 1.0
    for axis_at, shards_of in cuts:
        steps = jax.random.uniform(jax.random.fold_in(jax.random.fold_in(own_key, 6), axis_at), (shards_of,), jnp.float32, smallest / len(cuts), high / len(cuts))
        factor_of = factor_of * jnp.repeat(jnp.exp(steps), shape[axis_at] // shards_of).reshape((-1,) + (1,) * (len(shape) - 1 - axis_at))
    return factor_of


def centred(rng, extent, deviation, reach, shards=(), kind=jnp.bfloat16):
    gain = level_of(rng, extent, shards, -0.22, 0.18) if shards else 1.0
    entries = jax.random.normal(rng, extent, jnp.float32) * deviation * gain
    return jnp.minimum(jnp.maximum(entries, -reach), reach).astype(kind)


def setup_inputs(seed: int = 0) -> dict:
    streams_of = jax.random.split(jax.random.key(seed), 23)
    replay = jnp.clip(1.0 * jax.random.uniform(streams_of[0], (R_TOTAL, FRAME * FRAME * STACK), jnp.float32) ** level_of(streams_of[0], (R_TOTAL, FRAME * FRAME * STACK), ((0, 32),), -0.2, 0.2), 0.0, 1.0).astype(jnp.bfloat16)
    send_index = touch_ends(jax.random.randint(streams_of[1], (DEVICES, DEVICES, CAP), 0, R_DEV), jax.random.fold_in(streams_of[1], 1), 0, R_DEV - 1).astype(jnp.int32)
    send_count = draw_send_count(jax.random.fold_in(streams_of[22], 71), 0)
    actions = touch_ends(jax.random.randint(streams_of[3], (DEVICES, DEVICES, CAP), 0, ACTIONS), jax.random.fold_in(streams_of[3], 1), 0, ACTIONS - 1).astype(jnp.int32)
    game_ids = touch_ends(jax.random.randint(streams_of[4], (DEVICES, DEVICES, CAP), 0, GAMES), jax.random.fold_in(streams_of[4], 1), 0, GAMES - 1).astype(jnp.int32)
    legal_table = touch_ends((jax.random.randint(streams_of[5], (GAMES, ACTIONS), 0, 3) < 2).astype(jnp.int32), jax.random.fold_in(streams_of[5], 1), 0, 1)
    returns = centred(streams_of[6], (DEVICES, DEVICES, CAP), 1.0, 6.0, ((0, 32),), jnp.float32)
    bootstrap = centred(streams_of[7], (DEVICES, DEVICES, CAP), 1.0, 6.0, ((0, 32),), jnp.float32)
    is_weights = jnp.clip(jnp.exp(math.log(1.0) - 2.3025851 * jax.random.uniform(streams_of[8], (DEVICES, DEVICES, CAP), jnp.float32) ** level_of(streams_of[8], (DEVICES, DEVICES, CAP), ((0, 32),), -0.2, 0.2)), 0.1, 1.0)
    priority_table = draw_priority_table(jax.random.fold_in(streams_of[22], 71), 0)
    conv1_w = centred(streams_of[10], (K1, K1, STACK, C1), (K1 * K1 * STACK) ** -0.5, 0.375)
    conv1_b = centred(streams_of[11], (C1,), 0.3, 1.5)
    conv2_w = centred(streams_of[12], (K2, K2, C1, C2), (K2 * K2 * C1) ** -0.5, 0.25)
    conv2_b = centred(streams_of[13], (C2,), 0.3, 1.5)
    conv3_w = centred(streams_of[14], (K3, K3, C2, C3), (K3 * K3 * C2) ** -0.5, 0.25)
    conv3_b = centred(streams_of[15], (C3,), 0.3, 1.5)
    dense_w = centred(streams_of[16], (FLAT, HIDDEN_SIZE), FLAT ** -0.5, 0.109375)
    dense_b = centred(streams_of[17], (HIDDEN_SIZE,), 0.3, 1.5)
    value_w = centred(streams_of[18], (HIDDEN_SIZE, 1), HIDDEN_SIZE ** -0.5, 0.25)
    value_b = centred(streams_of[19], (1,), 0.3, 1.5)
    advantage_w = centred(streams_of[20], (HIDDEN_SIZE, ACTIONS), HIDDEN_SIZE ** -0.5, 0.25)
    advantage_b = centred(streams_of[21], (ACTIONS,), 0.3, 1.5)
    return {"replay": replay, "send_index": send_index, "send_count": send_count, "actions": actions, "game_ids": game_ids, "legal_table": legal_table, "returns": returns, "bootstrap": bootstrap, "is_weights": is_weights, "priority_table": priority_table, "conv1_w": conv1_w, "conv1_b": conv1_b, "conv2_w": conv2_w, "conv2_b": conv2_b, "conv3_w": conv3_w, "conv3_b": conv3_b, "dense_w": dense_w, "dense_b": dense_b, "value_w": value_w, "value_b": value_b, "advantage_w": advantage_w, "advantage_b": advantage_b}


GAMMA_THREE = 0.970299

@jax.custom_vjp
def low(v):
    return lax.optimization_barrier(v.astype(jnp.bfloat16)).astype(jnp.float32)

@jax.custom_vjp
def low_back(v):
    return v

def low_keep(v):
    return (low(v), None)

def low_pass(kept, grad):
    return (grad,)

def back_keep(v):
    return (v, None)

def back_low(kept, grad):
    return (low(grad),)
low.defvjp(low_keep, low_pass)
low_back.defvjp(back_keep, back_low)

def convolve(source, kernel, stride):
    return lax.conv_general_dilated(source, kernel, (stride, stride), 'VALID', dimension_numbers=('NHWC', 'HWIO', 'NHWC'), precision=lax.Precision.HIGHEST)

def huber(td_error):
    magnitude = jnp.abs(td_error)
    return jnp.where(magnitude <= 1.0, 0.5 * td_error * td_error, magnitude - 0.5)

def network(params, frames):
    conv1_w, conv1_b, conv2_w, conv2_b, conv3_w, conv3_b, dense_w, dense_b, value_w, value_b, advantage_w, advantage_b = params
    row_count = frames.shape[0]
    pictures = frames.reshape(row_count, FRAME, FRAME, STACK)
    pre_one = low_back(convolve(pictures, conv1_w, S1) + conv1_b)
    act_one = low(jax.nn.silu(pre_one))
    pre_two = low_back(convolve(act_one, conv2_w, S2) + conv2_b)
    act_two = low(jax.nn.silu(pre_two))
    pre_three = low_back(convolve(act_two, conv3_w, S3) + conv3_b)
    act_three = low(jax.nn.silu(pre_three)).reshape(row_count, FLAT)
    pre_dense = low_back(jnp.dot(act_three, dense_w, precision=lax.Precision.HIGHEST) + dense_b)
    act_dense = low(jax.nn.silu(pre_dense))
    head_w = jnp.concatenate([value_w, advantage_w], 1)
    head_b = jnp.concatenate([value_b, advantage_b], 0)
    return low_back(jnp.dot(act_dense, head_w, precision=lax.Precision.HIGHEST) + head_b)

def reference(replay, send_index, send_count, actions, game_ids, legal_table, returns, bootstrap, is_weights, priority_table, conv1_w, conv1_b, conv2_w, conv2_b, conv3_w, conv3_b, dense_w, dense_b, value_w, value_b, advantage_w, advantage_b):
    weights = (conv1_w, conv1_b, conv2_w, conv2_b, conv3_w, conv3_b, dense_w, dense_b, value_w, value_b, advantage_w, advantage_b)
    params = tuple((piece.astype(jnp.float32) for piece in weights))
    owners = jnp.arange(DEVICES, dtype=jnp.int32)
    noop_mask = (jnp.arange(ACTIONS, dtype=jnp.int32) == 0).astype(jnp.float32)
    legal_rows = jnp.maximum(legal_table.astype(jnp.float32), noop_mask[None, :])
    targets = returns + GAMMA_THREE * bootstrap
    slots_live = (jnp.arange(CAP, dtype=jnp.int32)[None, None, :] < jnp.transpose(send_count)[:, :, None]).astype(jnp.float32)
    rows_all = owners[None, :, None] * R_DEV + jnp.transpose(send_index, (1, 0, 2)).astype(jnp.int32)

    def block(params, learner):
        row_ids = rows_all[learner].reshape(-1)
        frames = jnp.take(replay, row_ids, axis=0).astype(jnp.float32)
        head = network(params, frames)
        state_value = head[:, :1]
        advantage = head[:, 1:]
        legal_mask = legal_rows[game_ids[learner].reshape(-1)]
        centre = lax.optimization_barrier(jnp.sum(advantage * legal_mask, 1)) / lax.optimization_barrier(jnp.sum(legal_mask, 1))
        q_part = state_value + advantage - centre[:, None]
        act_pick = (actions[learner].reshape(-1)[:, None] == jnp.arange(ACTIONS, dtype=jnp.int32)[None, :]).astype(jnp.float32)
        td_error = targets[learner].reshape(-1) - lax.optimization_barrier(jnp.sum(q_part * act_pick, 1))
        scaled = slots_live[learner].reshape(-1) * is_weights[learner].reshape(-1)
        return (jnp.sum(scaled * huber(td_error)) / SLOTS_DEV, (q_part, td_error))

    def total(params):

        def advance(running, learner):
            part, kept = jax.checkpoint(block)(params, learner)
            return (running + part, kept)
        return lax.scan(advance, jnp.zeros((), jnp.float32), owners)
    loss, pullback, (q_values, td_errors) = jax.vjp(total, params, has_aux=True)
    grads = pullback(jnp.ones_like(loss))[0]
    priority = ((td_errors * td_errors + 1.0) ** 0.3).reshape(DEVICES, DEVICES, CAP)
    candidates = jnp.where(slots_live > 0, priority, 0.0)
    fresh = jnp.zeros((R_TOTAL,), jnp.float32).at[rows_all.reshape(-1)].max(candidates.reshape(-1))
    new_table = jnp.where(fresh > 0.0, fresh, priority_table)
    top_priority = jnp.max(new_table)
    return (q_values, loss, grads[0], grads[1], grads[2], grads[3], grads[4], grads[5], grads[6], grads[7], grads[8], grads[9], grads[10], grads[11], new_table, top_priority)
```

```python
import jax
import jax.numpy as jnp
from jax import lax
from jax.sharding import PartitionSpec as P

FRAME = 84
STACK = 4
S1 = 4
S2 = 2
S3 = 1


GAMMA_THREE = 0.970299
PLAIN_SPEC = ("NHWC", "HWIO", "NHWC")


def forward_conv(source, kernel, stride):
    return lax.conv_general_dilated(
        source,
        kernel,
        (stride, stride),
        "VALID",
        dimension_numbers=PLAIN_SPEC,
        preferred_element_type=jnp.float32,
    )


def kernel_grad(source, upstream, stride):
    return lax.conv_general_dilated(
        source,
        upstream,
        (1, 1),
        "VALID",
        rhs_dilation=(stride, stride),
        dimension_numbers=("CHWN", "IHWO", "HWNC"),
        preferred_element_type=jnp.float32,
    )


def source_grad(upstream, kernel, stride):
    margin = kernel.shape[0] - 1
    return lax.conv_general_dilated(
        upstream,
        jnp.flip(kernel, (0, 1)),
        (1, 1),
        ((margin, margin), (margin, margin)),
        lhs_dilation=(stride, stride),
        dimension_numbers=("NHWC", "HWOI", "NHWC"),
        preferred_element_type=jnp.float32,
    )


def silu_slope(pre_value):
    gate_value = jax.nn.sigmoid(pre_value)
    return gate_value * (1.0 + pre_value * (1.0 - gate_value))


def huber(td_error):
    magnitude = jnp.abs(td_error)
    return jnp.where(magnitude <= 1.0, 0.5 * td_error * td_error, magnitude - 0.5)


def transposed_dot(left_side, right_side):
    return lax.dot_general(
        left_side, right_side, (((0,), (0,)), ((), ())), preferred_element_type=jnp.float32
    )


def learn(pictures, meta, own_index, own_live, legal_table, params):
    (
        conv1_w,
        conv1_b,
        conv2_w,
        conv2_b,
        conv3_w,
        conv3_b,
        dense_w,
        dense_b,
        value_w,
        value_b,
        advantage_w,
        advantage_b,
    ) = params
    row_count = pictures.shape[0]
    slot_count = own_index.shape[0]
    action_rows, game_rows, target_rows, weight_rows = meta
    head_w = jnp.concatenate([value_w, advantage_w], 1)
    head_b = jnp.concatenate([value_b, advantage_b], 0).astype(jnp.float32)
    game_count = legal_table.shape[0]
    action_count = legal_table.shape[1]
    noop_mask = (jnp.arange(action_count) == 0).astype(jnp.float32)
    legal_rows = jnp.maximum(legal_table.astype(jnp.float32), noop_mask[None, :])
    row_pick = (own_index[:, None] == jnp.arange(row_count)[None, :]).astype(jnp.float32)

    pre_one = forward_conv(pictures, conv1_w, S1) + conv1_b.astype(jnp.float32)
    act_one = jax.nn.silu(pre_one).astype(jnp.bfloat16)
    pre_two = forward_conv(act_one, conv2_w, S2) + conv2_b.astype(jnp.float32)
    act_two = jax.nn.silu(pre_two).astype(jnp.bfloat16)
    pre_three = forward_conv(act_two, conv3_w, S3) + conv3_b.astype(jnp.float32)
    act_three = jax.nn.silu(pre_three).astype(jnp.bfloat16)
    flat_three = act_three.reshape(row_count, -1)
    pre_dense = jnp.dot(
        flat_three, dense_w, preferred_element_type=jnp.float32
    ) + dense_b.astype(jnp.float32)
    act_dense = jax.nn.silu(pre_dense).astype(jnp.bfloat16)
    head_rows = jnp.dot(act_dense, head_w, preferred_element_type=jnp.float32) + head_b
    head_out = jnp.dot(row_pick, head_rows, precision=lax.Precision.HIGHEST)
    state_value = head_out[:, :1]
    advantage = head_out[:, 1:]
    game_pick = (game_rows[:, None] == jnp.arange(game_count)[None, :]).astype(jnp.float32)
    legal_mask = jnp.dot(game_pick, legal_rows, precision=lax.Precision.HIGHEST)
    counted = jnp.sum(legal_mask, 1)
    centre = jnp.sum(advantage * legal_mask, 1) / counted
    q_part = state_value + advantage - centre[:, None]
    act_pick = (action_rows[:, None] == jnp.arange(action_count)[None, :]).astype(jnp.float32)
    td_error = target_rows - jnp.sum(q_part * act_pick, 1)
    scaled = own_live * weight_rows
    loss = jnp.sum(scaled * huber(td_error)) / slot_count
    grad_taken = -scaled * jnp.clip(td_error, -1.0, 1.0) / slot_count
    grad_q = grad_taken[:, None] * act_pick
    grad_value = jnp.sum(grad_q, 1, keepdims=True)
    grad_adv = grad_q - legal_mask * (jnp.sum(grad_q, 1) / counted)[:, None]
    grad_head = jnp.concatenate([grad_value, grad_adv], 1).astype(jnp.bfloat16).astype(jnp.float32)
    grad_head = lax.dot_general(
        row_pick, grad_head, (((0,), (0,)), ((), ())), precision=lax.Precision.HIGHEST
    )
    head_w_grad = lax.dot_general(
        act_dense.astype(jnp.float32), grad_head, (((0,), (0,)), ((), ())), precision=lax.Precision.HIGHEST
    )
    head_b_grad = jnp.sum(grad_head, 0)
    up_dense = lax.dot_general(
        grad_head, head_w.astype(jnp.float32), (((1,), (1,)), ((), ())), precision=lax.Precision.HIGHEST
    )
    grad_dense = (up_dense * silu_slope(pre_dense)).astype(jnp.bfloat16)
    dense_w_grad = transposed_dot(flat_three, grad_dense)
    dense_b_grad = jnp.sum(grad_dense.astype(jnp.float32), 0)
    up_three = lax.dot_general(
        grad_dense, dense_w, (((1,), (1,)), ((), ())), preferred_element_type=jnp.float32
    ).reshape(act_three.shape)
    grad_three = (up_three * silu_slope(pre_three)).astype(jnp.bfloat16)
    conv3_w_grad = kernel_grad(act_two, grad_three, S3)
    conv3_b_grad = jnp.sum(grad_three.astype(jnp.float32), (0, 1, 2))
    up_two = source_grad(grad_three, conv3_w, S3)
    grad_two = (up_two * silu_slope(pre_two)).astype(jnp.bfloat16)
    conv2_w_grad = kernel_grad(act_one, grad_two, S2)
    conv2_b_grad = jnp.sum(grad_two.astype(jnp.float32), (0, 1, 2))
    up_one = source_grad(grad_two, conv2_w, S2)
    grad_one = (up_one * silu_slope(pre_one)).astype(jnp.bfloat16)
    conv1_w_grad = kernel_grad(pictures, grad_one, S1)
    conv1_b_grad = jnp.sum(grad_one.astype(jnp.float32), (0, 1, 2))
    grads = (
        conv1_w_grad,
        conv1_b_grad,
        conv2_w_grad,
        conv2_b_grad,
        conv3_w_grad,
        conv3_b_grad,
        dense_w_grad,
        dense_b_grad,
        head_w_grad[:, :1],
        head_b_grad[:1],
        head_w_grad[:, 1:],
        head_b_grad[1:],
    )
    return q_part, td_error, loss, grads


def per_device(
    replay,
    send_index,
    send_count,
    actions,
    game_ids,
    legal_table,
    returns,
    bootstrap,
    is_weights,
    priority_table,
    *params,
):
    axes = ("hst", "dev")
    peer_count = send_index.shape[1]
    capacity = send_index.shape[2]
    own_index = send_index[0].reshape(-1)
    own_live = (
        jnp.arange(capacity, dtype=jnp.int32)[None, :] < send_count[0][:, None]
    ).astype(jnp.float32).reshape(-1)
    targets = returns[0] + GAMMA_THREE * bootstrap[0]
    outgoing = jnp.stack(
        [actions[0].astype(jnp.float32), game_ids[0].astype(jnp.float32), targets, is_weights[0]], 1
    )
    meta = lax.all_to_all(outgoing, axes, split_axis=0, concat_axis=0, tiled=True)
    meta = (
        meta[:, 0].reshape(-1).astype(jnp.int32),
        meta[:, 1].reshape(-1).astype(jnp.int32),
        meta[:, 2].reshape(-1),
        meta[:, 3].reshape(-1),
    )
    pictures = replay.reshape(replay.shape[0], FRAME, FRAME, STACK)
    q_part, td_rows, loss_local, grads = learn(
        pictures, meta, own_index, own_live, legal_table, params
    )
    q_values = lax.all_to_all(
        q_part.reshape(peer_count, capacity, -1), axes, split_axis=0, concat_axis=0, tiled=True
    ).reshape(1, peer_count * capacity, -1)
    totals = lax.psum((loss_local,) + grads, axes)
    candidates = own_live * ((td_rows * td_rows + 1.0) ** 0.3)
    fresh = jnp.max(
        jnp.where(own_index[:, None] == jnp.arange(replay.shape[0])[None, :], candidates[:, None], 0.0), 0
    )
    new_table = jnp.where(fresh > 0.0, fresh, priority_table)
    top_priority = lax.pmax(jnp.max(new_table), axes)
    return (q_values,) + totals + (new_table, top_priority)


def solution(mesh):
    placed = (
        P(("hst", "dev"), None),
        P(("hst", "dev"), None, None),
        P(("hst", "dev"), None),
        P(("hst", "dev"), None, None),
        P(("hst", "dev"), None, None),
        P(),
        P(("hst", "dev"), None, None),
        P(("hst", "dev"), None, None),
        P(("hst", "dev"), None, None),
        P(("hst", "dev")),
        P(),
        P(),
        P(),
        P(),
        P(),
        P(),
        P(),
        P(),
        P(),
        P(),
        P(),
        P(),
    )
    return jax.shard_map(
        per_device,
        mesh=mesh,
        in_specs=placed,
        out_specs=(
            P(("hst", "dev"), None, None),
            P(),
            P(),
            P(),
            P(),
            P(),
            P(),
            P(),
            P(),
            P(),
            P(),
            P(),
            P(),
            P(),
            P(("hst", "dev")),
            P(),
        ),
        check_vma=False,
    )
```

```python
import functools

import jax
import jax.numpy as jnp
from jax import lax
from jax.experimental import pallas as pl
from jax.experimental.pallas import tpu as pltpu
from jax.sharding import PartitionSpec as P

GAMMA_THREE = 0.970299
ACTIONS = 18
FLAT = 3136
HIDDEN = 512
CHUNKS = 11
MESH = pl.DeviceIdType.MESH
F32=jnp.float32; BF=jnp.bfloat16
NN=(((1,),(0,)),((),())); NT=(((1,),(1,)),((),())); TN=(((0,),(0,)),((),()))

def dot(a,b,dims=NN):
    return lax.dot_general(a,b,dims,preferred_element_type=F32)
def iota(shape,axis): return lax.broadcasted_iota(jnp.int32,shape,axis)
def tile_lanes(w,width,times,keep,dims=NN):
    n=width*times
    e=((iota((width,n),1)%width==iota((width,n),0)) & (iota((width,n),1)<keep*width)).astype(BF)
    return dot(w,e,dims)

def build_toeplitz(w1,w2,w3,t1,t2a,t2b,t2c,t3a,t3b,u2,u3):
    lane32=iota((16,256),1)//32
    wt1=tile_lanes(w1[...],32,8,7)
    for kr in range(8):
        lo=wt1[32*kr:32*kr+16]; hi=wt1[32*kr+16:32*kr+32]
        for b in range(8):
            t1[pl.ds(128*kr+16*b,16),:]=(jnp.where(lane32==b,lo,0.0)+jnp.where(lane32==b-1,hi,0.0)).astype(BF)
    lane64=iota((32,256),1)//64
    wt2=tile_lanes(w2[...],64,4,4)
    def blk2(kr,p,n,cl):
        col=7*p+cl
        out=jnp.zeros((32,256),F32)
        if cl>=(7 if p<2 else 6): return out
        for kc in range(4):
            if (col-kc)%2: continue
            j=(col-kc)//2
            if 0<=j<9 and 4*n<=j<4*n+4:
                out=out+jnp.where(lane64==j-4*n,wt2[(4*kr+kc)*32:(4*kr+kc)*32+32],0.0)
        return out
    for kr in range(4):
        for cl in range(8):
            for ref,pairs in ((t2a,((0,0),(1,0))),(t2b,((1,1),(2,1)))):
                for k,(p,n) in enumerate(pairs):
                    ref[pl.ds(512*kr+256*k+32*cl,32),:]=blk2(kr,p,n,cl).astype(BF)
            t2c[pl.ds(256*kr+32*cl,32),:]=blk2(kr,2,2,cl)[:,:128].astype(BF)
    lane64b=iota((64,256),1)//64
    wt3=tile_lanes(w3[...],64,4,4)
    def blk3(kr,t,m,cl):
        col=4*t+cl
        out=jnp.zeros((64,256),F32)
        if col>8: return out
        for kc in range(3):
            j=col-kc
            if 0<=j<7 and 4*m<=j<4*m+4:
                out=out+jnp.where(lane64b==j-4*m,wt3[(3*kr+kc)*64:(3*kr+kc)*64+64],0.0)
        return out
    for kr in range(3):
        for cl in range(4):
            t3a[pl.ds(512*kr+64*cl,64),:]=blk3(kr,0,0,cl).astype(BF)
            t3a[pl.ds(512*kr+256+64*cl,64),:]=blk3(kr,1,0,cl).astype(BF)
            t3b[pl.ds(384*kr+64*cl,64),:]=blk3(kr,1,1,cl).astype(BF)
            if cl<2:
                t3b[pl.ds(384*kr+256+64*cl,64),:]=blk3(kr,2,1,cl).astype(BF)
    lane32c=iota((64,256),1)//32
    wx2=[[tile_lanes(w2[pl.ds((4*kr+kc)*32,32),:],32,8,8,TN) for kc in range(4)] for kr in range(4)]
    def ublk2(kr,p,j):
        out=jnp.zeros((64,256),F32)
        if j>8: return out
        for kc in range(4):
            cl=2*j+kc-7*p
            if 0<=cl<(7 if p<2 else 6):
                out=out+jnp.where(lane32c==cl,wx2[kr][kc],0.0)
        return out
    for par in range(2):
        for k2 in range(2):
            kr=par+2*k2
            for jl in range(4):
                u2[par,pl.ds(256*k2+64*jl,64),:]=ublk2(kr,0,jl).astype(BF)
            for j in range(8):
                u2[par,pl.ds(512+512*k2+64*j,64),:]=ublk2(kr,1,j).astype(BF)
            for jl in range(6):
                u2[par,pl.ds(1536+384*k2+64*jl,64),:]=ublk2(kr,2,4+jl).astype(BF)
    wx3=[[tile_lanes(w3[pl.ds((3*kr+kc)*64,64),:],64,4,4,TN) for kc in range(3)] for kr in range(3)]
    def ublk3(kr,t,j):
        out=jnp.zeros((64,256),F32)
        if j>6: return out
        for kc in range(3):
            cl=j+kc-4*t
            if 0<=cl<4 and j+kc<=8:
                out=out+jnp.where(lane64b==cl,wx3[kr][kc],0.0)
        return out
    for kr in range(3):
        for jl in range(4):
            u3[pl.ds(256*kr+64*jl,64),:]=ublk3(kr,0,jl).astype(BF)
        for j in range(8):
            u3[pl.ds(768+512*kr+64*j,64),:]=ublk3(kr,1,j).astype(BF)
        for jl in range(4):
            u3[pl.ds(2304+256*kr+64*jl,64),:]=ublk3(kr,2,4+jl).astype(BF)

def gates(pre):
    s=1.0/(1.0+jnp.exp(-pre))
    return pre*s, s*(1.0+pre*(1.0-s))

def relayout(x, x3, base):
    keep = iota((128, 128), 1) < 112
    for r in range(8):
        for p in range(3):
            at = r * 336 + 112 * p
            if at + 128 <= 2688:
                v = x[at:at + 128, :]
            else:
                v = jnp.concatenate([x[at:2688, :], jnp.zeros((at + 128 - 2688, 128), BF)], 0)
            v = v.T
            if p == 2:
                v = jnp.where(keep, v, jnp.zeros_like(v))
            x3[base + r, :, 128 * p:128 * p + 128] = v

def conv1_rows(c,x3,t1,bias,a1,s1):
    L=[]
    for q in range(2):
        for p in range(3):
            L.append(jnp.concatenate([x3[8*c+4*q+kr,:,128*p:128*p+128] for kr in range(8)],axis=1))
    pre=dot(jnp.concatenate(L,axis=0),t1[...])+bias[:,0:256]
    act,slope=gates(pre)
    for q in range(2):
        for p in range(3):
            k=(3*q+p)*128
            a1[2*c+q,:,256*p:256*p+256]=act[k:k+128].astype(BF)
            s1[2*c+q,:,256*p:256*p+256]=slope[k:k+128]

def conv2_all(a1,t2a,t2b,t2c,bias,a2,s2):
    def step(s,_):
        rows=[[a1[2*(3*s+q)+kr+1] for kr in range(4)] for q in range(3)]
        def lhs(lo,hi):
            return jnp.concatenate([jnp.concatenate([rows[q][kr][:,lo:hi] for kr in range(4)],1) for q in range(3)],0)
        for (lo,hi,w,o0,o1) in ((0,512,t2a,0,256),(256,768,t2b,256,512),(512,768,t2c,512,640)):
            pre=dot(lhs(lo,hi),w[...])+bias[:,256+o0:256+o1]
            act,slope=gates(pre)
            for q in range(3):
                a2[3*s+q,:,o0:o1]=act[128*q:128*q+128].astype(BF)
                s2[3*s+q,:,o0:o1]=slope[128*q:128*q+128]
        return 0
    lax.fori_loop(0,3,step,0)

def conv3_all(a2,t3a,t3b,bias,a3,s3):
    for i0,n in ((0,4),(4,3)):
        for lo,hi,w,o0 in ((0,512,t3a,0),(256,640,t3b,256)):
            L=jnp.concatenate([jnp.concatenate([a2[i0+q+kr][:,lo:hi] for kr in range(3)],1) for q in range(n)],0)
            pre=dot(L,w[...])+bias[:,896+o0:896+o0+256]
            act,slope=gates(pre)
            if o0: slope=jnp.where(iota((128*n,256),1)<192,slope,0.0)
            for q in range(n):
                a3[i0+q,:,o0:o0+256]=act[128*q:128*q+128].astype(BF)
                s3[i0+q,:,o0:o0+256]=slope[128*q:128*q+128]

def dense_head(a3,dw,hw,bias):
    pre=bias[:,1408:1920]
    for r in range(7):
        pre=pre+dot(a3[r],dw[pl.ds(448*r,512),:])
    act,slope=gates(pre)
    act4=act.astype(BF)
    head=dot(act4,hw[...],NT)+bias[:,1920:2048]
    return act4,slope,head

def split2(v):
    hi=v.astype(BF); return hi,(v-hi.astype(F32)).astype(BF)
def split3(v):
    hi=v.astype(BF); r=v-hi.astype(F32); mid=r.astype(BF); return hi,mid,(r-mid.astype(F32)).astype(BF)

def td_part(head,meta,local,legal,table,slots,live_slots):
    lane=iota((slots,128),1)
    idx=local[:,4:5].astype(jnp.int32); live=local[:,5:6]
    action=meta[:,0:1].astype(jnp.int32); game=meta[:,1:2].astype(jnp.int32)
    target=meta[:,2:3]; weight=meta[:,3:4]
    pick=lane==idx
    pickb=pick.astype(F32).astype(BF)
    h=None
    for part in split3(head):
        d=dot(pickb,part); h=d if h is None else h+d
    game_pick=(lane==game).astype(F32).astype(BF)
    mask=dot(game_pick,legal,NT)
    counted=jnp.sum(mask,1,keepdims=True)
    centre=jnp.sum(h*mask,1,keepdims=True)/counted
    q=h[:,ACTIONS:ACTIONS+1]+h-centre
    act_pick=(lane==action).astype(F32)
    td=target-jnp.sum(q*act_pick,1,keepdims=True)
    scaled=live*weight
    mag=jnp.abs(td)
    hub=jnp.where(mag<=1.0,0.5*td*td,mag-0.5)
    loss=jnp.sum(scaled*hub,0,keepdims=True)/live_slots
    gt=-scaled*jnp.clip(td,-1.0,1.0)/live_slots
    G=(gt*(act_pick+(lane==ACTIONS).astype(F32))-mask*(gt/counted)).astype(BF)
    pr=live*jnp.exp(0.3*jnp.log(td*td+1.0))
    fresh=jnp.max(jnp.where(pick,pr,0.0),0,keepdims=True)
    newt=jnp.where(fresh>0.0,fresh,table)
    top=jnp.max(newt,1,keepdims=True)
    grow=dot(pickb,G,TN)
    dhb=jnp.sum(G.astype(F32),0,keepdims=True)
    return q,grow,dhb,loss,newt,top

def head_grads(grow,act4,slope4,hw):
    hi,lo=split2(grow)
    up4=dot(hi,hw[...])+dot(lo,hw[...])
    dhw=dot(hi,act4,TN)+dot(lo,act4,TN)
    g4=(up4*slope4).astype(BF)
    return g4,dhw

def g3_all(g4,dw,s3,g3):
    z=jnp.zeros((128,512),BF)
    for r in (0,1,9,10): g3[r]=z
    b3=None
    for r in range(7):
        up=dot(g4,dw[pl.ds(448*r,512),:],NT)
        g=(up*s3[r]).astype(BF)
        g3[r+2]=g
        b=g.astype(F32); b3=b if b3 is None else b3+b
    return jnp.sum(b3,0,keepdims=True)

def fold64(row):
    n=row.shape[1]//128
    t=row[:,0:128]
    for k in range(1,n): t=t+row[:,128*k:128*k+128]
    return t+pltpu.roll(t,64,1)

def conv3_dw(a2,g3,sp,base):
    low=iota((64,128),1)<64
    G=jnp.concatenate([g3[r+2] for r in range(7)],0)
    def lhs(lo,hi):
        return jnp.concatenate([jnp.concatenate([a2[i+kr][:,lo:hi] for kr in range(3)],1) for i in range(7)],0)
    d0=dot(G[:,0:256],lhs(0,512),TN)
    d1=dot(G[:,256:512],lhs(256,640),TN)
    for kr in range(3):
        E0=E1=O0=O1=None
        for j in range(7):
            def T(ct):
                if j<4: return d0[64*j:64*j+64,512*kr+128*ct:512*kr+128*ct+128]
                return d1[64*(j-4):64*(j-4)+64,384*kr+128*(ct-2):384*kr+128*(ct-2)+128]
            add=lambda a,b: b if a is None else a+b
            if j%2==0:
                E0=add(E0,T(j//2)); E1=add(E1,T(j//2+1))
            else:
                O0=add(O0,T(j//2)); O1=add(O1,T(j//2+1))
        o0=pltpu.roll(O0,64,1); o1=pltpu.roll(O1,64,1)
        sp[pl.ds(base+128*kr,64),:]=E0+jnp.where(low,o0,o1)
        sp[pl.ds(base+128*kr+64,64),:]=E1+o1

def conv3_dx(g3,u3,s2,g2):
    z=jnp.zeros((128,640),BF)
    g2[0]=z; g2[10]=z
    def step(s,tot):
        rows=[[g3[3*s+q+2-kr] for kr in range(3)] for q in range(3)]
        def lhs(lo,hi):
            return jnp.concatenate([jnp.concatenate([rows[q][kr][:,lo:hi] for kr in range(3)],1) for q in range(3)],0)
        outs=[]
        for (lo,hi,k0,k1,o0,o1) in ((0,256,0,768,0,256),(0,512,768,2304,256,512),(256,512,2304,3072,512,640)):
            up=dot(lhs(lo,hi),u3[pl.ds(k0,k1-k0),0:o1-o0])
            acc=None
            for q in range(3):
                g=(up[128*q:128*q+128]*s2[3*s+q,:,o0:o1]).astype(BF)
                g2[3*s+q+1,:,o0:o1]=g
                f=g.astype(F32); acc=f if acc is None else acc+f
            outs.append(jnp.sum(acc,0,keepdims=True))
        return tot+jnp.concatenate(outs,1)
    return lax.fori_loop(0,3,step,jnp.zeros((1,640),F32))

def conv2_dw(a1,g2,sp,base):
    lane=iota((64,128),1)//32
    G=jnp.concatenate([g2[i+1] for i in range(9)],0)
    for kr in range(4):
        L=jnp.concatenate([a1[2*i+kr+1] for i in range(9)],0)
        d=[dot(G[:,0:256],L[:,0:512],TN),dot(G[:,256:512],L[:,256:768],TN),dot(G[:,512:640],L[:,512:768],TN)]
        lo=[0,1,2]
        tot=jnp.zeros((64,128),F32)
        for j in range(9):
            n=j//4
            kc=0
            while kc<4:
                col=2*j+kc; p=min(col//7,2); cl=col-7*p
                lim=7 if p<2 else 6
                cnt=min(4-kc,lim-cl)
                v=d[n][64*(j-4*n):64*(j-4*n)+64,256*(p-lo[n]):256*(p-lo[n])+256]
                sh=(32*(kc-cl))%256
                if sh: v=pltpu.roll(v,sh,1)
                v=v[:,0:128]
                tot=tot+(v if cnt==4 else jnp.where((lane>=kc)&(lane<kc+cnt),v,0.0))
                kc+=cnt
        sp[pl.ds(base+64*kr,64),:]=tot

def conv2_dx(g2,u2,s1,g1):
    def step(t,tot):
        a0=5*(t//2); par=t%2
        def lhs(lo,hi):
            return jnp.concatenate([jnp.concatenate([g2[a0+q+1][:,lo:hi],g2[a0+q][:,lo:hi]],1) for q in range(5)],0)
        outs=[]
        for p,(lo,hi,k0,k1) in enumerate(((0,256,0,512),(0,512,512,1536),(256,640,1536,2304))):
            up=dot(lhs(lo,hi),u2[par,pl.ds(k0,k1-k0),:])
            acc=None
            for q in range(5):
                r=2*(a0+q)+par
                g=(up[128*q:128*q+128]*s1[r+1,:,256*p:256*p+256]).astype(BF)
                g1[r+1,:,256*p:256*p+256]=g
                f=g.astype(F32); acc=f if acc is None else acc+f
            outs.append(jnp.sum(acc,0,keepdims=True))
        return tot+outs[0]+outs[1]+outs[2]
    return lax.fori_loop(0,4,step,jnp.zeros((1,256),F32))

def conv1_dw(x3,g1,acc,sp,base):
    acc[...]=jnp.zeros_like(acc)
    def step(s,_):
        Ls=[];Gs=[]
        for q in range(4):
            for p in range(3):
                Gs.append(g1[4*s+q+1,:,256*p:256*p+256])
                Ls.append(jnp.concatenate([x3[4*(4*s+q)+kr+4,:,128*p:128*p+128] for kr in range(8)],axis=1))
        acc[...]+=dot(jnp.concatenate(Gs,0),jnp.concatenate(Ls,0),TN)
        return 0
    lax.fori_loop(0,5,step,0)
    lane=iota((32,128),1)//32
    for a in range(2):
        out=jnp.zeros((32,128),F32)
        for qq in range(4):
            kr=4*a+qq
            tot=None
            for j in range(7):
                v=acc[pl.ds(32*j,32),128*kr:128*kr+128]
                sh=(32*qq-16*j)%128
                if sh: v=pltpu.roll(v,sh,1)
                tot=v if tot is None else tot+v
            out=out+jnp.where(lane==qq,tot,0.0)
        sp[pl.ds(base+32*a,32),:]=out


def expand_bias(pack, bias):
    def tiled(width):
        e = (iota((128, 256), 1) % width == iota((128, 256), 0)).astype(F32).astype(BF)
        return dot(pack[...], e)
    lane = iota((1, 256), 1)
    zero = jnp.zeros((1, 256), F32)
    t32, t64 = tiled(32), tiled(64)
    bias[:, 0:256] = jnp.where(lane < 224, t32[0:1], zero)
    bias[:, 256:512] = t64[1:2]
    bias[:, 512:768] = t64[1:2]
    bias[:, 768:896] = jnp.where(lane < 64, t64[1:2], zero)[:, 0:128]
    bias[:, 896:1152] = t64[2:3]
    bias[:, 1152:1408] = jnp.where(lane < 192, t64[2:3], zero)
    wide = pack[...].astype(F32)
    for k in range(5):
        bias[:, 1408 + 128 * k:1536 + 128 * k] = wide[3 + k:4 + k]


def prepare_heads(value, advantage, legal, stage, head_w, legal_t):
    stage[...] = jnp.zeros_like(stage)
    stage[0:ACTIONS, :] = advantage[...].astype(F32)
    stage[ACTIONS:ACTIONS + 1, :] = value[...].astype(F32)
    head_w[...] = stage[...].astype(BF)
    stage[...] = jnp.zeros_like(stage)
    stage[0:ACTIONS, 0:legal.shape[1]] = legal[...].astype(F32)
    row = iota((128, 128), 0)
    legal_t[...] = jnp.where(row == 0, 1.0, stage[:, 0:128]).astype(BF)


def prepare_meta(act, game, ret, boot, weight, index, count, stage, meta_out):
    cap, peers = act.shape
    stage[:, 0:128] = jnp.zeros((128, 128), F32)
    fields = (
        act[...].astype(F32),
        game[...].astype(F32),
        ret[...] + GAMMA_THREE * boot[...],
        weight[...],
        index[...].astype(F32),
        (iota((cap, peers), 0) < count[...]).astype(F32),
    )
    for k, field in enumerate(fields):
        stage[8 * k:8 * k + cap, 0:peers] = field
    by_peer = stage[:, 0:128].T
    rows = 8 * peers
    repeat = (iota((rows, 128), 1) == iota((rows, 128), 0) // 8).astype(F32).astype(BF)
    spread = sum(dot(repeat, part) for part in split3(by_peer))
    spread = jnp.where(iota((rows, 128), 0) % 8 == iota((rows, 128), 1) % 8, spread, 0.0)
    collect = (iota((128, 128), 0) // 8 == iota((128, 128), 1)).astype(F32).astype(BF)
    meta_out[...] = sum(dot(part, collect) for part in split3(spread))


def learner_kernel(
    sizes,
    x, act, game, ret, boot, weight, index, count, table, legal, w1, w2, w3, pack, value, advantage, dense_in,
    dg_out, sp_out, q_out, tab_out,
    x3, a1, s1, a2, s2, a3, s3, g3, g2, dw, t1, t2a, t2b, t2c, t3a, t3b, u2, u3, acc,
    bias, stage, head_w, legal_t, meta_out, meta_in, q_send, q_in, a3t, a_in, g4_send, g4_in,
    part, z_in, dg, sp, sp_in, sp_mid, sp_z, sp_all,
    dw_sem, out_sem, meta_s, meta_r, q_s, q_r, a_s, a_r, af_s, af_r, b_s, b_r, rs_s, rs_r,
    az_s, az_r, ap_s, ap_r, ad_s, ad_r, ac_s, ac_r, p1_s, p1_r, p2_s, p2_r, p3_s, p3_r,
):
    hsize, dsize, zrows = sizes
    zsize = dsize // 2
    peers = hsize * dsize
    region = zrows * zsize
    step_at = pl.program_id(0)
    h = lax.axis_index("hst")
    d = lax.axis_index("dev")
    z = d // 2
    core = d % 2
    mine = 2 * h + core
    me = h * dsize + d

    def where_is(peer):
        return (peer // dsize, peer % dsize)

    def send(src, dst, s_sem, r_sem, device):
        copy = pltpu.make_async_remote_copy(
            src_ref=src, dst_ref=dst, send_sem=s_sem, recv_sem=r_sem, device_id=device, device_id_type=MESH
        )
        copy.start()

    def landed(dst, r_sem, s_sem):
        pltpu.make_async_remote_copy(
            src_ref=dst, dst_ref=dst, send_sem=s_sem, recv_sem=r_sem, device_id=(h, d), device_id_type=MESH
        ).wait_recv()

    def sent(src, s_sem, r_sem):
        pltpu.make_async_remote_copy(
            src_ref=src, dst_ref=src, send_sem=s_sem, recv_sem=r_sem, device_id=(h, d), device_id_type=MESH
        ).wait_send()

    @pl.when(step_at == 0)
    def _():
        barrier = pltpu.get_barrier_semaphore()

        def greet(k, carry):
            pl.semaphore_signal(
                barrier, inc=1, device_id=where_is((me + k) % peers), device_id_type=MESH
            )
            return carry

        lax.fori_loop(1, peers, greet, 0)
        pltpu.make_async_copy(dense_in, dw.at[pl.ds(0, FLAT)], dw_sem).start()
        dw[pl.ds(FLAT, 64)] = jnp.zeros((64, HIDDEN), BF)
        build_toeplitz(w1, w2, w3, t1, t2a, t2b, t2c, t3a, t3b, u2, u3)
        expand_bias(pack, bias)
        prepare_heads(value, advantage, legal, stage, head_w, legal_t)
        prepare_meta(act, game, ret, boot, weight, index, count, stage, meta_out)

    relayout(x, x3, 8 * step_at + 4)
    conv1_rows(step_at, x3, t1, bias, a1, s1)

    @pl.when(step_at == 1)
    def _():
        pl.semaphore_wait(pltpu.get_barrier_semaphore(), peers - 1)

        def give(k, carry):
            peer = (me + k) % peers
            send(
                meta_out.at[pl.ds(pl.multiple_of(8 * peer, 8), 8)],
                meta_in.at[pl.ds(pl.multiple_of(8 * me, 8), 8)],
                meta_s.at[k], meta_r.at[k], where_is(peer),
            )
            return carry

        lax.fori_loop(1, peers, give, 0)

    def partial(half):
        for k in range(1, 2 * hsize):
            src = (mine - k + 2 * hsize) % (2 * hsize)
            landed(g4_in.at[half, src], b_r.at[half, k], b_s.at[half, k])
        left = jnp.concatenate([a_in[j] for j in range(2 * hsize)], 1)
        right = jnp.concatenate([g4_in[half, j] for j in range(2 * hsize)], 0)
        part[half, 0:784] = dot(left, right)
        for k in range(1, zsize):
            to = (z + k) % zsize
            send(
                part.at[half, pl.ds(pl.multiple_of(zrows * to, 16), zrows)], z_in.at[half, z],
                rs_s.at[half, k], rs_r.at[half, k], (h, 2 * to + core),
            )
        z_in[half, z] = part[half, pl.ds(pl.multiple_of(zrows * z, 16), zrows)]

    last = step_at == CHUNKS - 1
    sibling = (h, 2 * z + 1 - core)
    own_rows = pl.ds(pl.multiple_of(784 * h, 16), 784)
    row_me = pl.ds(pl.multiple_of(8 * me, 8), 8)

    @pl.when(last)
    def _():
        conv2_all(a1, t2a, t2b, t2c, bias, a2, s2)
        conv3_all(a2, t3a, t3b, bias, a3, s3)
        for r in range(7):
            a3t[pl.ds(448 * r, 448), :] = a3[r].T[0:448]

        for k in range(1, hsize):
            to = (h + k) % hsize
            send(
                a3t.at[pl.ds(pl.multiple_of(784 * to, 16), 784)], a_in.at[mine], a_s.at[k], a_r.at[k], (to, d)
            )
        send(a3t.at[own_rows], a_in.at[mine], af_s.at[0], af_r.at[0], sibling)

    @pl.when(last)
    def _():
        pltpu.make_async_copy(dense_in, dw.at[pl.ds(0, FLAT)], dw_sem).wait()
        act4, slope4, head = dense_head(a3, dw, head_w, bias)

        def take(k, carry):
            peer = (me - k + peers) % peers
            landed(meta_in.at[pl.ds(pl.multiple_of(8 * peer, 8), 8)], meta_r.at[k], meta_s.at[k])
            return carry

        lax.fori_loop(1, peers, take, 0)
        meta_in[row_me, :] = meta_out[row_me, :]
        q, grow, dhb, loss, newt, top = td_part(
            head, meta_in[...], meta_out[...], legal_t[...], table[...], 8 * peers, float(sizes_slots(sizes, act))
        )
        tab_out[...] = jnp.broadcast_to(newt, (8, 128))
        lane = iota((8 * peers, 128), 1)
        q_send[...] = jnp.where(lane == 19, top, jnp.where(lane == 20, loss, q))
        g4, dhw = head_grads(grow, act4, slope4, head_w)
        for quarter in range(4):
            g4_send[quarter] = g4[:, 128 * quarter:128 * quarter + 128]
        for half in range(2):
            for k in range(1, 2 * hsize):
                to = (mine + k) % (2 * hsize)
                send(
                    g4_send.at[2 * (to % 2) + half], g4_in.at[half, mine], b_s.at[half, k], b_r.at[half, k],
                    (to // 2, 2 * z + to % 2),
                )
        for half in range(2):
            g4_in[half, mine] = g4_send[2 * core + half]
        a_in[mine] = a3t[own_rows, :]

        def answer(k, carry):
            peer = (me + k) % peers
            send(
                q_send.at[pl.ds(pl.multiple_of(8 * peer, 8), 8)],
                q_in.at[pl.ds(pl.multiple_of(8 * me, 8), 8)],
                q_s.at[k], q_r.at[k], where_is(peer),
            )
            return carry

        lax.fori_loop(1, peers, answer, 0)
        q_in[row_me, :] = q_send[row_me, :]

        for k in range(4):
            sp[pl.ds(704 + 24 * k, 24), :] = dhw[0:24, 128 * k:128 * k + 128]
        b4 = jnp.sum(g4.astype(F32), 0, keepdims=True)
        for k in range(4):
            sp[803 + k:804 + k, :] = b4[:, 128 * k:128 * k + 128]
        sp[807:808, :] = dhb
        sp[808:832, :] = jnp.zeros((24, 128), F32)
        sp[802:803, :] = fold64(g3_all(g4, dw, s3, g3))

    @pl.when(last)
    def _():
        conv3_dw(a2, g3, sp, 320)

    @pl.when(last)
    def _():
        sp[801:802, :] = fold64(conv3_dx(g3, u3, s2, g2))

        for k in range(1, hsize):
            src = 2 * ((h - k + hsize) % hsize) + core
            landed(a_in.at[src], a_r.at[k], a_s.at[k])
            send(a_in.at[src], a_in.at[src], af_s.at[k], af_r.at[k], sibling)

    @pl.when(last)
    def _():
        conv2_dw(a1, g2, sp, 64)

    @pl.when(last)
    def _():

        for k in range(hsize):
            src = 2 * ((h - k + hsize) % hsize) + 1 - core
            landed(a_in.at[src], af_r.at[k], af_s.at[k])

        for half in range(2):
            part[half, 784:region] = jnp.zeros((region - 784, 128), F32)
        partial(0)

    @pl.when(last)
    def _():
        b1 = conv2_dx(g2, u2, s1, a1)
        b1 = b1[:, 0:128] + b1[:, 128:256]
        b1 = b1 + pltpu.roll(b1, 64, 1)
        sp[800:801, :] = b1 + pltpu.roll(b1, 32, 1)

    @pl.when(last)
    def _():
        partial(1)

    @pl.when(last)
    def _():
        conv1_dw(x3, a1, acc, sp, 0)

    @pl.when(last)
    def _():

        group = 832 // (2 * hsize)

        def group_rows(j):
            return pl.ds(pl.multiple_of(group * j, 8), group)

        for k in range(1, 2 * hsize):
            to = (mine + k) % (2 * hsize)
            send(sp.at[group_rows(to)], sp_in.at[mine], p1_s.at[k], p1_r.at[k], (to // 2, 2 * z + to % 2))

        hy, hx = h // 2, h % 2
        flip_x, flip_y = 2 * hy + 1 - hx, 2 * (1 - hy) + hx
        near = (1 - core) * flip_x + core * flip_y
        far = (1 - core) * flip_y + core * flip_x
        across = 3 - h

        def place(half, hh, zz, cc):
            rows = pl.multiple_of(region * hh + zrows * zz, 16)
            lanes = pl.multiple_of(256 * cc + 128 * half, 128)
            return dg.at[pl.ds(rows, zrows), pl.ds(lanes, 128)]

        def spread(half, zz, k):
            at = place(half, h, zz, core)
            send(at, at, ap_s.at[half, 0, k], ap_r.at[half, 0, k], (near, d))
            send(at, at, ap_s.at[half, 1, k], ap_r.at[half, 1, k], (far, d))
            send(at, at, ac_s.at[half, 0, k], ac_r.at[half, 0, k], sibling)

        def finish(half):
            for k in range(1, zsize):
                landed(z_in.at[half, (z - k + zsize) % zsize], rs_r.at[half, k], rs_s.at[half, k])
            total = z_in[half, 0]
            for j in range(1, zsize):
                total = total + z_in[half, j]
            rows = pl.multiple_of(region * h + zrows * z, 16)
            lanes = pl.multiple_of(256 * core + 128 * half, 128)
            dg[pl.ds(rows, zrows), pl.ds(lanes, 128)] = total.astype(BF)
            at = place(half, h, z, core)
            for k in range(1, zsize):
                send(at, at, az_s.at[half, k], az_r.at[half, k], (h, 2 * ((z + k) % zsize) + core))
            spread(half, z, 0)

        def pass_on(half):
            for k in range(1, zsize):
                zz = (z - k + zsize) % zsize
                landed(place(half, h, zz, core), az_r.at[half, k], az_s.at[half, k])
                spread(half, zz, k)

        def pass_across(half):
            for k in range(zsize):
                zz = (z - k + zsize) % zsize
                at = place(half, near, zz, core)
                landed(at, ap_r.at[half, 0, k], ap_s.at[half, 0, k])
                send(at, at, ad_s.at[half, k], ad_r.at[half, k], (far, d))
                send(at, at, ac_s.at[half, 1, k], ac_r.at[half, 1, k], sibling)
                at = place(half, far, zz, core)
                landed(at, ap_r.at[half, 1, k], ap_s.at[half, 1, k])
                send(at, at, ac_s.at[half, 2, k], ac_r.at[half, 2, k], sibling)

        def pass_last(half):
            for k in range(zsize):
                zz = (z - k + zsize) % zsize
                at = place(half, across, zz, core)
                landed(at, ad_r.at[half, k], ad_s.at[half, k])
                send(at, at, ac_s.at[half, 3, k], ac_r.at[half, 3, k], sibling)

        def gather_core(half):
            other = 1 - core
            near_o = core * flip_x + (1 - core) * flip_y
            far_o = core * flip_y + (1 - core) * flip_x
            for k in range(zsize):
                zz = (z - k + zsize) % zsize
                for j, hh in enumerate((h, near_o, far_o, across)):
                    landed(place(half, hh, zz, other), ac_r.at[half, j, k], ac_s.at[half, j, k])

        finish(0)

        sp_in[mine] = sp[group_rows(mine), :]
        for k in range(1, 2 * hsize):
            src = (mine - k + 2 * hsize) % (2 * hsize)
            landed(sp_in.at[src], p1_r.at[k], p1_s.at[k])
        total = sp_in[0]
        for j in range(1, 2 * hsize):
            total = total + sp_in[j]
        sp_mid[...] = total
        sp_z[z] = total
        for k in range(1, zsize):
            to = (z + k) % zsize
            send(sp_mid, sp_z.at[z], p2_s.at[k], p2_r.at[k], (h, 2 * to + core))

        finish(1)
        pass_on(0)
        for k in range(1, zsize):
            landed(sp_z.at[(z - k + zsize) % zsize], p2_r.at[k], p2_s.at[k])
        total = sp_z[0]
        for j in range(1, zsize):
            total = total + sp_z[j]
        sp_all[group_rows(mine), :] = total
        for k in range(1, 2 * hsize):
            to = (mine + k) % (2 * hsize)
            send(
                sp_all.at[group_rows(mine)], sp_all.at[group_rows(mine)], p3_s.at[k], p3_r.at[k],
                (to // 2, 2 * z + to % 2),
            )
        pass_on(1)
        pass_across(0)
        pass_across(1)
        pass_last(0)
        pass_last(1)
        for k in range(1, 2 * hsize):
            src = (mine - k + 2 * hsize) % (2 * hsize)
            landed(sp_all.at[group_rows(src)], p3_r.at[k], p3_s.at[k])

        def receive(k, carry):
            peer = (me - k + peers) % peers
            landed(q_in.at[pl.ds(pl.multiple_of(8 * peer, 8), 8)], q_r.at[k], q_s.at[k])
            return carry

        lax.fori_loop(1, peers, receive, 0)
        gather_core(0)
        gather_core(1)

        def drain(k, carry):
            sent(meta_out.at[pl.ds(0, 8)], meta_s.at[k], meta_r.at[k])
            sent(q_send.at[pl.ds(0, 8)], q_s.at[k], q_r.at[k])
            return carry

        lax.fori_loop(1, peers, drain, 0)
        for k in range(1, hsize):
            sent(a_in.at[mine], a_s.at[k], a_r.at[k])
        for k in range(hsize):
            sent(a_in.at[mine], af_s.at[k], af_r.at[k])
        for k in range(1, 2 * hsize):
            sent(sp_in.at[mine], p1_s.at[k], p1_r.at[k])
            sent(sp_in.at[mine], p3_s.at[k], p3_r.at[k])
        for k in range(1, zsize):
            sent(sp_mid, p2_s.at[k], p2_r.at[k])
        for half in range(2):
            for k in range(1, 2 * hsize):
                sent(g4_in.at[half, mine], b_s.at[half, k], b_r.at[half, k])
            for k in range(1, zsize):
                sent(z_in.at[half, z], rs_s.at[half, k], rs_r.at[half, k])
                sent(place(half, h, z, core), az_s.at[half, k], az_r.at[half, k])
            for k in range(zsize):
                at = place(half, h, z, core)
                for j in range(2):
                    sent(at, ap_s.at[half, j, k], ap_r.at[half, j, k])
                sent(at, ad_s.at[half, k], ad_r.at[half, k])
                for j in range(4):
                    sent(at, ac_s.at[half, j, k], ac_r.at[half, j, k])

        copies = [
            pltpu.make_async_copy(src, dst, out_sem.at[k])
            for k, (src, dst) in enumerate(((dg, dg_out), (sp_all, sp_out), (q_in, q_out)))
        ]
        for copy in copies:
            copy.start()
        for copy in copies:
            copy.wait()


def sizes_slots(sizes, act):
    return sizes[0] * sizes[1] * act.shape[0]


def learner(sizes, args, cap):
    hsize, dsize, zrows = sizes
    zsize, peers = dsize // 2, hsize * dsize
    region = zrows * zsize
    dma = pltpu.SemaphoreType.DMA
    vmem = pltpu.VMEM
    groups = 2 * hsize
    scratch = [
        vmem((92, 128, 384), BF), vmem((22, 128, 768), BF), vmem((22, 128, 768), F32), vmem((9, 128, 640), BF),
        vmem((9, 128, 640), F32), vmem((7, 128, 512), BF), vmem((7, 128, 512), F32), vmem((11, 128, 512), BF),
        vmem((11, 128, 640), BF), vmem((3200, 512), BF), vmem((1024, 256), BF), vmem((2048, 256), BF),
        vmem((2048, 256), BF), vmem((1024, 128), BF), vmem((1536, 256), BF), vmem((1152, 256), BF),
        vmem((2, 2304, 256), BF), vmem((3072, 256), BF), vmem((256, 1024), F32),
        vmem((1, 2048), F32), vmem((128, 512), F32), vmem((128, 512), BF), vmem((128, 128), BF),
        vmem((8 * peers, 128), F32), vmem((8 * peers, 128), F32), vmem((8 * peers, 128), F32),
        vmem((8 * peers, 128), F32), vmem((FLAT, 128), BF), vmem((groups, 784, 128), BF), vmem((4, 128, 128), BF),
        vmem((2, groups, 128, 128), BF), vmem((2, region, 128), F32), vmem((2, zsize, zrows, 128), F32),
        vmem((hsize * region, 512), BF), vmem((832, 128), F32), vmem((groups, 832 // groups, 128), F32),
        vmem((832 // groups, 128), F32), vmem((zsize, 832 // groups, 128), F32), vmem((832, 128), F32),
        dma, dma((3,)), dma((peers,)), dma((peers,)), dma((peers,)), dma((peers,)),
        dma((hsize,)), dma((hsize,)), dma((hsize,)), dma((hsize,)), dma((2, groups)), dma((2, groups)),
        dma((2, zsize)), dma((2, zsize)), dma((2, zsize)), dma((2, zsize)),
        dma((2, 2, zsize)), dma((2, 2, zsize)), dma((2, zsize)), dma((2, zsize)),
        dma((2, 4, zsize)), dma((2, 4, zsize)), dma((groups,)), dma((groups,)), dma((zsize,)), dma((zsize,)),
        dma((groups,)), dma((groups,)),
    ]
    whole = pl.BlockSpec(memory_space=pltpu.VMEM)
    outside = pl.BlockSpec(memory_space=pl.ANY)
    return pl.pallas_call(
        functools.partial(learner_kernel, sizes),
        grid=(CHUNKS,),
        in_specs=[pl.BlockSpec((2688, 128), lambda c: (c, 0))] + [whole] * 15 + [outside],
        out_specs=[outside, outside, outside, whole],
        out_shape=[
            jax.ShapeDtypeStruct((hsize * region, 512), BF),
            jax.ShapeDtypeStruct((832, 128), F32),
            jax.ShapeDtypeStruct((8 * peers, 128), F32),
            jax.ShapeDtypeStruct((8, 128), F32),
        ],
        scratch_shapes=scratch,
        compiler_params=pltpu.CompilerParams(collective_id=0, has_side_effects=True, vmem_limit_bytes=63 << 20),
    )(*args)


def output_kernel(dg, sp, q, tab, dense, c1, c2, c3, bias1, bias2, bias3, bias4, vw, vb, aw, ab, loss, top, table):
    dense[...] = dg[0:784].astype(F32)

    @pl.when(pl.program_id(0) == 0)
    def _():
        for a in range(2):
            c1[pl.ds(128 * a, 128), :] = sp[pl.ds(32 * a, 32), :].T
        for kr in range(4):
            c2[pl.ds(128 * kr, 128), :] = sp[pl.ds(64 + 64 * kr, 64), :].T
        for kr in range(3):
            c3[pl.ds(192 * kr, 128), :] = sp[pl.ds(320 + 128 * kr, 64), :].T
            c3[pl.ds(192 * kr + 128, 64), :] = sp[pl.ds(384 + 128 * kr, 64), :].T[0:64]
        bias1[...] = sp[800:801, 0:32]
        bias2[...] = sp[801:802, 0:64]
        bias3[...] = sp[802:803, 0:64]
        for k in range(4):
            bias4[:, 128 * k:128 * k + 128] = sp[803 + k:804 + k, :]
            heads = sp[pl.ds(704 + 24 * k, 24), :]
            aw[:, 128 * k:128 * k + 128] = heads[0:ACTIONS]
            vw[:, 128 * k:128 * k + 128] = heads[ACTIONS:ACTIONS + 1]
        ab[...] = sp[807:808, 0:ACTIONS]
        vb[...] = sp[807:808, ACTIONS:ACTIONS + 1]
        rows = q[...]
        top[...] = jnp.max(rows[:, 19:20], 0, keepdims=True)
        first = iota((rows.shape[0], 1), 0) % 8 == 0
        loss[...] = jnp.sum(jnp.where(first, rows[:, 20:21], 0.0), 0, keepdims=True)
        table[...] = tab[0:1, :]


def outputs(sizes, dg, sp, q, tab):
    hsize, dsize, zrows = sizes
    region = zrows * (dsize // 2)
    whole = pl.BlockSpec(memory_space=pltpu.VMEM)
    shapes = (
        (FLAT, 512), (256, 32), (512, 64), (576, 64), (1, 32), (1, 64), (1, 64), (1, 512), (1, 512), (1, 1),
        (ACTIONS, 512), (1, ACTIONS), (1, 1), (1, 1), (1, 128),
    )
    return pl.pallas_call(
        output_kernel,
        grid=(hsize,),
        in_specs=[pl.BlockSpec((region, 512), lambda k: (k, 0)), whole, whole, whole],
        out_specs=[pl.BlockSpec((784, 512), lambda k: (k, 0))] + [whole] * 14,
        out_shape=[jax.ShapeDtypeStruct(s, F32) for s in shapes],
    )(dg, sp, q, tab)


def per_device(
    hsize,
    dsize,
    replay,
    send_index,
    send_count,
    actions,
    game_ids,
    legal_table,
    returns,
    bootstrap,
    is_weights,
    priority_table,
    conv1_w,
    conv1_b,
    conv2_w,
    conv2_b,
    conv3_w,
    conv3_b,
    dense_w,
    dense_b,
    value_w,
    value_b,
    advantage_w,
    advantage_b,
):
    cap = send_index.shape[2]
    peers = hsize * dsize
    zsize = dsize // 2
    zrows = -(-784 // (16 * zsize)) * 16
    sizes = (hsize, dsize, zrows)
    gap = functools.partial(jnp.zeros, dtype=BF)
    pack = jnp.concatenate(
        [conv1_b, gap(96), conv2_b, gap(64), conv3_b, gap(64), dense_b, advantage_b, value_b, gap(109)]
    ).reshape(8, 128)
    args = (
        replay.T,
        actions[0].T,
        game_ids[0].T,
        returns[0].T,
        bootstrap[0].T,
        is_weights[0].T,
        send_index[0].T,
        send_count,
        priority_table.reshape(1, -1),
        legal_table.T,
        conv1_w.reshape(256, 32),
        conv2_w.reshape(512, 64),
        conv3_w.reshape(576, 64),
        pack,
        value_w.T,
        advantage_w.T,
        dense_w,
    )
    dg, sp, q, tab = learner(sizes, args, cap)
    (dense, c1, c2, c3, b1, b2, b3, b4, vw, vb, aw, ab, loss, top, table) = outputs(sizes, dg, sp, q, tab)
    q_values = q.reshape(peers, 8, 128)[:, :cap, :ACTIONS].reshape(1, peers * cap, ACTIONS)
    return (
        q_values,
        loss.reshape(()),
        c1.reshape(conv1_w.shape),
        b1.reshape(-1),
        c2.reshape(conv2_w.shape),
        b2.reshape(-1),
        c3.reshape(conv3_w.shape),
        b3.reshape(-1),
        dense,
        b4.reshape(-1),
        vw.T,
        vb.reshape(-1),
        aw.T,
        ab.reshape(-1),
        table.reshape(-1),
        top.reshape(()),
    )


def solution(mesh):
    both = ("hst", "dev")
    rows2, rows3 = P(both, None), P(both, None, None)
    placed = (rows2, rows3, rows2, rows3, rows3, P(), rows3, rows3, rows3, P(both)) + (P(),) * 12
    return jax.shard_map(
        functools.partial(per_device, mesh.shape["hst"], mesh.shape["dev"]),
        mesh=mesh,
        in_specs=placed,
        out_specs=(rows3,) + (P(),) * 13 + (P(both), P()),
        check_vma=False,
    )
```

```python
import functools

import jax
import jax.numpy as jnp
from jax import lax
from jax.experimental import pallas as pl
from jax.experimental.pallas import tpu as pltpu
from jax.sharding import PartitionSpec as P

GAMMA_THREE = 0.970299
ACTIONS = 18
FLAT = 3136
HIDDEN = 512
CHUNKS = 11
PIXELS = 2688
SLOTS = 4
MESH = pl.DeviceIdType.MESH
JOIN = (
    "meta", "q", "g4", "sum0", "sum1", "gather_core0", "gather_core1", "small", "small_z", "small_back", "small_all",
    "small_core", "late", "late_z", "late_all",
)
LEAVE = JOIN + (
    "act", "act_core", "gather_z0", "gather_z1", "gather_near0", "gather_near1", "gather_diag0", "gather_diag1",
)
ROWS = (416, 384)
START = (0, 400)
F32=jnp.float32; BF=jnp.bfloat16
NN=(((1,),(0,)),((),())); NT=(((1,),(1,)),((),())); TN=(((0,),(0,)),((),()))

def dot(a,b,dims=NN):
    return lax.dot_general(a,b,dims,preferred_element_type=F32)
def iota(shape,axis): return lax.broadcasted_iota(jnp.int32,shape,axis)
def tile_lanes(w,width,times,keep,dims=NN):
    n=width*times
    e=((iota((width,n),1)%width==iota((width,n),0)) & (iota((width,n),1)<keep*width)).astype(BF)
    return dot(w,e,dims)

def build_toeplitz(w1,w2,w3,t1,t2a,t2b,t2c,t3a,t3b):
    lane32=iota((16,256),1)//32
    wt1=tile_lanes(w1[...],32,8,7)
    for kr in range(8):
        lo=wt1[32*kr:32*kr+16]; hi=wt1[32*kr+16:32*kr+32]
        for b in range(8):
            t1[pl.ds(128*kr+16*b,16),:]=(jnp.where(lane32==b,lo,0.0)+jnp.where(lane32==b-1,hi,0.0)).astype(BF)
    lane64=iota((32,256),1)//64
    wt2=tile_lanes(w2[...],64,4,4)
    def blk2(kr,p,n,cl):
        col=7*p+cl
        out=jnp.zeros((32,256),F32)
        if cl>=(7 if p<2 else 6): return out
        for kc in range(4):
            if (col-kc)%2: continue
            j=(col-kc)//2
            if 0<=j<9 and 4*n<=j<4*n+4:
                out=out+jnp.where(lane64==j-4*n,wt2[(4*kr+kc)*32:(4*kr+kc)*32+32],0.0)
        return out
    for kr in range(4):
        for cl in range(8):
            for ref,pairs in ((t2a,((0,0),(1,0))),(t2b,((1,1),(2,1)))):
                for k,(p,n) in enumerate(pairs):
                    ref[pl.ds(512*kr+256*k+32*cl,32),:]=blk2(kr,p,n,cl).astype(BF)
            t2c[pl.ds(256*kr+32*cl,32),:]=blk2(kr,2,2,cl)[:,:128].astype(BF)
    lane64b=iota((64,256),1)//64
    wt3=tile_lanes(w3[...],64,4,4)
    def blk3(kr,t,m,cl):
        col=4*t+cl
        out=jnp.zeros((64,256),F32)
        if col>8: return out
        for kc in range(3):
            j=col-kc
            if 0<=j<7 and 4*m<=j<4*m+4:
                out=out+jnp.where(lane64b==j-4*m,wt3[(3*kr+kc)*64:(3*kr+kc)*64+64],0.0)
        return out
    for kr in range(3):
        for cl in range(4):
            t3a[pl.ds(512*kr+64*cl,64),:]=blk3(kr,0,0,cl).astype(BF)
            t3a[pl.ds(512*kr+256+64*cl,64),:]=blk3(kr,1,0,cl).astype(BF)
            t3b[pl.ds(384*kr+64*cl,64),:]=blk3(kr,1,1,cl).astype(BF)
            if cl<2:
                t3b[pl.ds(384*kr+256+64*cl,64),:]=blk3(kr,2,1,cl).astype(BF)

def build_transposed(w2,w3,u2,u3):
    lane64b=iota((64,256),1)//64
    lane32c=iota((64,256),1)//32
    wx2=[[tile_lanes(w2[pl.ds((4*kr+kc)*32,32),:],32,8,8,TN) for kc in range(4)] for kr in range(4)]
    def ublk2(kr,p,j):
        out=jnp.zeros((64,256),F32)
        if j>8: return out
        for kc in range(4):
            cl=2*j+kc-7*p
            if 0<=cl<(7 if p<2 else 6):
                out=out+jnp.where(lane32c==cl,wx2[kr][kc],0.0)
        return out
    for par in range(2):
        for k2 in range(2):
            kr=par+2*k2
            for jl in range(4):
                u2[par,pl.ds(256*k2+64*jl,64),:]=ublk2(kr,0,jl).astype(BF)
            for j in range(8):
                u2[par,pl.ds(512+512*k2+64*j,64),:]=ublk2(kr,1,j).astype(BF)
            for jl in range(6):
                u2[par,pl.ds(1536+384*k2+64*jl,64),:]=ublk2(kr,2,4+jl).astype(BF)
    wx3=[[tile_lanes(w3[pl.ds((3*kr+kc)*64,64),:],64,4,4,TN) for kc in range(3)] for kr in range(3)]
    def ublk3(kr,t,j):
        out=jnp.zeros((64,256),F32)
        if j>6: return out
        for kc in range(3):
            cl=j+kc-4*t
            if 0<=cl<4 and j+kc<=8:
                out=out+jnp.where(lane64b==cl,wx3[kr][kc],0.0)
        return out
    for kr in range(3):
        for jl in range(4):
            u3[pl.ds(256*kr+64*jl,64),:]=ublk3(kr,0,jl).astype(BF)
        for j in range(8):
            u3[pl.ds(768+512*kr+64*j,64),:]=ublk3(kr,1,j).astype(BF)
        for jl in range(4):
            u3[pl.ds(2304+256*kr+64*jl,64),:]=ublk3(kr,2,4+jl).astype(BF)

def gates(pre):
    s=1.0/(1.0+jnp.exp(-pre))
    return pre*s, s*(1.0+pre*(1.0-s))

def relayout(x, x3, base, rows=8):
    keep = iota((128, 128), 1) < 112
    for r in range(rows):
        for p in range(3):
            at = r * 336 + 112 * p
            if at + 128 <= 336 * rows:
                v = x[at:at + 128, :]
            else:
                v = jnp.concatenate([x[at:336 * rows, :], jnp.zeros((at + 128 - 336 * rows, 128), BF)], 0)
            v = v.T
            if p == 2:
                v = jnp.where(keep, v, jnp.zeros_like(v))
            x3[base + r, :, 128 * p:128 * p + 128] = v

def conv1_rows(c,x3,t1,bias,a1,s1,which=(0,1)):
    L=[]
    for q in which:
        for p in range(3):
            L.append(jnp.concatenate([x3[8*c+4*q+kr,:,128*p:128*p+128] for kr in range(8)],axis=1))
    pre=dot(jnp.concatenate(L,axis=0),t1[...])+bias[:,0:256]
    act,slope=gates(pre)
    for q in which:
        for p in range(3):
            k=(3*(q-which[0])+p)*128
            a1[2*c+q,:,256*p:256*p+256]=act[k:k+128].astype(BF)
            s1[2*c+q,:,256*p:256*p+256]=slope[k:k+128]

def conv2_all(a1,t2a,t2b,t2c,bias,a2,s2):
    rows=[[a1[2*(q)+kr+1] for kr in range(4)] for q in range(9)]
    def lhs(lo,hi):
        return jnp.concatenate([jnp.concatenate([rows[q][kr][:,lo:hi] for kr in range(4)],1) for q in range(9)],0)
    for (lo,hi,w,o0,o1) in ((0,512,t2a,0,256),(256,768,t2b,256,512),(512,768,t2c,512,640)):
        pre=dot(lhs(lo,hi),w[...])+bias[:,256+o0:256+o1]
        act,slope=gates(pre)
        for q in range(9):
            a2[q,:,o0:o1]=act[128*q:128*q+128].astype(BF)
            s2[q,:,o0:o1]=slope[128*q:128*q+128]

def conv3_all(a2,t3a,t3b,bias,a3,s3):
    for i0,n in ((0,4),(4,3)):
        for lo,hi,w,o0 in ((0,512,t3a,0),(256,640,t3b,256)):
            L=jnp.concatenate([jnp.concatenate([a2[i0+q+kr][:,lo:hi] for kr in range(3)],1) for q in range(n)],0)
            pre=dot(L,w[...])+bias[:,896+o0:896+o0+256]
            act,slope=gates(pre)
            if o0: slope=jnp.where(iota((128*n,256),1)<192,slope,0.0)
            for q in range(n):
                a3[i0+q,:,o0:o0+256]=act[128*q:128*q+128].astype(BF)
                s3[i0+q,:,o0:o0+256]=slope[128*q:128*q+128]

def dense_head(a3,dw,hw,bias):
    pre=bias[:,1408:1920]
    for r in range(7):
        pre=pre+dot(a3[r],dw[pl.ds(448*r,512),:])
    act,slope=gates(pre)
    act4=act.astype(BF)
    head=dot(act4,hw[...],NT)+bias[:,1920:2048]
    return act4,slope,head

def split2(v):
    hi=v.astype(BF); return hi,(v-hi.astype(F32)).astype(BF)
def split3(v):
    hi=v.astype(BF); r=v-hi.astype(F32); mid=r.astype(BF); return hi,mid,(r-mid.astype(F32)).astype(BF)

def td_part(head,meta,local,legal,table,slots,live_slots):
    lane=iota((slots,128),1)
    idx=local[:,4:5].astype(jnp.int32); live=local[:,5:6]
    action=meta[:,0:1].astype(jnp.int32); game=meta[:,1:2].astype(jnp.int32)
    target=meta[:,2:3]; weight=meta[:,3:4]
    pick=lane==idx
    pickb=pick.astype(F32).astype(BF)
    h=None
    for part in split3(head):
        d=dot(pickb,part); h=d if h is None else h+d
    game_pick=(lane==game).astype(F32).astype(BF)
    mask=dot(game_pick,legal,NT)
    counted=jnp.sum(mask,1,keepdims=True)
    centre=jnp.sum(h*mask,1,keepdims=True)/counted
    q=h[:,ACTIONS:ACTIONS+1]+h-centre
    act_pick=(lane==action).astype(F32)
    td=target-jnp.sum(q*act_pick,1,keepdims=True)
    scaled=live*weight
    mag=jnp.abs(td)
    hub=jnp.where(mag<=1.0,0.5*td*td,mag-0.5)
    loss=jnp.sum(scaled*hub,0,keepdims=True)/live_slots
    gt=-scaled*jnp.clip(td,-1.0,1.0)/live_slots
    G=(gt*(act_pick+(lane==ACTIONS).astype(F32))-mask*(gt/counted)).astype(BF)
    pr=live*jnp.exp(0.3*jnp.log(td*td+1.0))
    fresh=jnp.max(jnp.where(pick,pr,0.0),0,keepdims=True)
    newt=jnp.where(fresh>0.0,fresh,table)
    top=jnp.max(newt,1,keepdims=True)
    grow=dot(pickb,G,TN)
    dhb=jnp.sum(G.astype(F32),0,keepdims=True)
    return q,grow,dhb,loss,newt,top

def head_grads(grow,act4,slope4,hw):
    hi,lo=split2(grow)
    up4=dot(hi,hw[...])+dot(lo,hw[...])
    dhw=dot(hi,act4,TN)+dot(lo,act4,TN)
    g4=(up4*slope4).astype(BF)
    return g4,dhw

def g3_all(g4,dw,s3,g3):
    z=jnp.zeros((128,512),BF)
    for r in (0,1,9,10): g3[r]=z
    b3=None
    for r in range(7):
        up=dot(g4,dw[pl.ds(448*r,512),:],NT)
        g=(up*s3[r]).astype(BF)
        g3[r+2]=g
        b=g.astype(F32); b3=b if b3 is None else b3+b
    return jnp.sum(b3,0,keepdims=True)

def fold64(row):
    n=row.shape[1]//128
    t=row[:,0:128]
    for k in range(1,n): t=t+row[:,128*k:128*k+128]
    return t+pltpu.roll(t,64,1)

def conv3_dw(a2,g3,sp,base):
    low=iota((64,128),1)<64
    G=jnp.concatenate([g3[r+2] for r in range(7)],0)
    def lhs(lo,hi):
        return jnp.concatenate([jnp.concatenate([a2[i+kr][:,lo:hi] for kr in range(3)],1) for i in range(7)],0)
    d0=dot(G[:,0:256],lhs(0,512),TN)
    d1=dot(G[:,256:512],lhs(256,640),TN)
    for kr in range(3):
        E0=E1=O0=O1=None
        for j in range(7):
            def T(ct):
                if j<4: return d0[64*j:64*j+64,512*kr+128*ct:512*kr+128*ct+128]
                return d1[64*(j-4):64*(j-4)+64,384*kr+128*(ct-2):384*kr+128*(ct-2)+128]
            add=lambda a,b: b if a is None else a+b
            if j%2==0:
                E0=add(E0,T(j//2)); E1=add(E1,T(j//2+1))
            else:
                O0=add(O0,T(j//2)); O1=add(O1,T(j//2+1))
        o0=pltpu.roll(O0,64,1); o1=pltpu.roll(O1,64,1)
        sp[pl.ds(base+128*kr,64),:]=E0+jnp.where(low,o0,o1)
        sp[pl.ds(base+128*kr+64,64),:]=E1+o1

def conv3_dx(g3,u3,s2,g2):
    z=jnp.zeros((128,640),BF)
    g2[0]=z; g2[10]=z
    def step(s,tot):
        rows=[[g3[3*s+q+2-kr] for kr in range(3)] for q in range(3)]
        def lhs(lo,hi):
            return jnp.concatenate([jnp.concatenate([rows[q][kr][:,lo:hi] for kr in range(3)],1) for q in range(3)],0)
        outs=[]
        for (lo,hi,k0,k1,o0,o1) in ((0,256,0,768,0,256),(0,512,768,2304,256,512),(256,512,2304,3072,512,640)):
            up=dot(lhs(lo,hi),u3[pl.ds(k0,k1-k0),0:o1-o0])
            acc=None
            for q in range(3):
                g=(up[128*q:128*q+128]*s2[3*s+q,:,o0:o1]).astype(BF)
                g2[3*s+q+1,:,o0:o1]=g
                f=g.astype(F32); acc=f if acc is None else acc+f
            outs.append(jnp.sum(acc,0,keepdims=True))
        return tot+jnp.concatenate(outs,1)
    return lax.fori_loop(0,3,step,jnp.zeros((1,640),F32))

def conv2_dw(a1,g2,sp,base,first,last):
    lane=iota((64,128),1)//32
    G=jnp.concatenate([g2[i+1] for i in range(9)],0)
    for kr in range(first,last):
        L=jnp.concatenate([a1[2*i+kr+1] for i in range(9)],0)
        d=[dot(G[:,0:256],L[:,0:512],TN),dot(G[:,256:512],L[:,256:768],TN),dot(G[:,512:640],L[:,512:768],TN)]
        lo=[0,1,2]
        tot=jnp.zeros((64,128),F32)
        for j in range(9):
            n=j//4
            kc=0
            while kc<4:
                col=2*j+kc; p=min(col//7,2); cl=col-7*p
                lim=7 if p<2 else 6
                cnt=min(4-kc,lim-cl)
                v=d[n][64*(j-4*n):64*(j-4*n)+64,256*(p-lo[n]):256*(p-lo[n])+256]
                sh=(32*(kc-cl))%256
                if sh: v=pltpu.roll(v,sh,1)
                v=v[:,0:128]
                tot=tot+(v if cnt==4 else jnp.where((lane>=kc)&(lane<kc+cnt),v,0.0))
                kc+=cnt
        sp[pl.ds(base+64*kr,64),:]=tot

def conv2_dx(g2,u2,s1,g1,first,last):
    def step(t,tot):
        a0=5*(t//2); par=t%2
        def lhs(lo,hi):
            return jnp.concatenate([jnp.concatenate([g2[a0+q+1][:,lo:hi],g2[a0+q][:,lo:hi]],1) for q in range(5)],0)
        outs=[]
        for p,(lo,hi,k0,k1) in enumerate(((0,256,0,512),(0,512,512,1536),(256,640,1536,2304))):
            up=dot(lhs(lo,hi),u2[par,pl.ds(k0,k1-k0),:])
            acc=None
            for q in range(5):
                r=2*(a0+q)+par
                g=(up[128*q:128*q+128]*s1[r+1,:,256*p:256*p+256]).astype(BF)
                g1[r+1,:,256*p:256*p+256]=g
                f=g.astype(F32); acc=f if acc is None else acc+f
            outs.append(jnp.sum(acc,0,keepdims=True))
        return tot+outs[0]+outs[1]+outs[2]
    return lax.fori_loop(first,last,step,jnp.zeros((1,256),F32))

def conv1_dw(x3,g1,acc,first,last):
    if first==0: acc[...]=jnp.zeros_like(acc)
    def step(s,_):
        Ls=[];Gs=[]
        for q in range(4):
            for p in range(3):
                Gs.append(g1[4*s+q+1,:,256*p:256*p+256])
                Ls.append(jnp.concatenate([x3[4*(4*s+q)+kr+4,:,128*p:128*p+128] for kr in range(8)],axis=1))
        acc[...]+=dot(jnp.concatenate(Gs,0),jnp.concatenate(Ls,0),TN)
        return 0
    lax.fori_loop(first,last,step,0)

def conv1_fold(acc,sp,base):
    lane=iota((32,128),1)//32
    for a in range(2):
        out=jnp.zeros((32,128),F32)
        for qq in range(4):
            kr=4*a+qq
            tot=None
            for j in range(7):
                v=acc[pl.ds(32*j,32),128*kr:128*kr+128]
                sh=(32*qq-16*j)%128
                if sh: v=pltpu.roll(v,sh,1)
                tot=v if tot is None else tot+v
            out=out+jnp.where(lane==qq,tot,0.0)
        sp[pl.ds(base+32*a,32),:]=out


def to_fixed(v):
    top = jnp.maximum(jnp.max(jnp.abs(v), 0, keepdims=True), 1e-30)
    e = jnp.ceil(jnp.log(top) * 1.4426950408889634)
    code = jnp.clip(jnp.round(v * jnp.exp((15.0 - e) * 0.6931471805599453)), -32767.0, 32767.0)
    return code.astype(jnp.int32).astype(jnp.int16), jnp.broadcast_to(e, (16, 128)).astype(jnp.int32).astype(jnp.int16)

def from_fixed(code, e):
    scale = jnp.exp((e.astype(jnp.int32).astype(F32)[0:1] - 15.0) * 0.6931471805599453)
    return code.astype(jnp.int32).astype(F32) * scale


def expand_bias(raw, stage, pack, bias):
    c1, c2, c3, dense, value, advantage = raw
    stage[...] = jnp.zeros_like(stage)
    stage[0:1, 0:32] = c1[...].astype(F32)
    stage[1:2, 0:64] = c2[...].astype(F32)
    stage[2:3, 0:64] = c3[...].astype(F32)
    stage[3:7, 0:128] = dense[...].astype(F32)
    stage[7:8, 0:ACTIONS] = advantage[...].astype(F32)
    heads = jnp.where(iota((1, 128), 1) == ACTIONS, value[...].astype(F32), stage[7:8, 0:128])
    stage[7:8, 0:128] = heads
    pack[...] = stage[0:8, 0:128].astype(BF)

    def tiled(width):
        e = (iota((128, 256), 1) % width == iota((128, 256), 0)).astype(F32).astype(BF)
        return dot(pack[...], e)
    lane = iota((1, 256), 1)
    zero = jnp.zeros((1, 256), F32)
    t32, t64 = tiled(32), tiled(64)
    bias[:, 0:256] = jnp.where(lane < 224, t32[0:1], zero)
    bias[:, 256:512] = t64[1:2]
    bias[:, 512:768] = t64[1:2]
    bias[:, 768:896] = jnp.where(lane < 64, t64[1:2], zero)[:, 0:128]
    bias[:, 896:1152] = t64[2:3]
    bias[:, 1152:1408] = jnp.where(lane < 192, t64[2:3], zero)
    wide = pack[...].astype(F32)
    for k in range(5):
        bias[:, 1408 + 128 * k:1536 + 128 * k] = wide[3 + k:4 + k]


def prepare_heads(value, advantage, legal, stage, head_w, legal_t):
    stage[...] = jnp.zeros_like(stage)
    stage[0:ACTIONS, :] = advantage[...].astype(F32)
    stage[ACTIONS:ACTIONS + 1, :] = value[...].astype(F32)
    head_w[...] = stage[...].astype(BF)
    stage[...] = jnp.zeros_like(stage)
    stage[0:ACTIONS, 0:legal.shape[1]] = legal[...].astype(F32)
    row = iota((128, 128), 0)
    legal_t[...] = jnp.where(row == 0, 1.0, stage[:, 0:128]).astype(BF)


def prepare_meta(act, game, ret, boot, weight, index, count, stage, meta_out):
    cap, peers = act.shape
    stage[:, 0:128] = jnp.zeros((128, 128), F32)
    fields = (
        act[...].astype(F32),
        game[...].astype(F32),
        ret[...] + GAMMA_THREE * boot[...],
        weight[...],
        index[...].astype(F32),
        (iota((cap, peers), 0) < count[...]).astype(F32),
    )
    for k, field in enumerate(fields):
        stage[8 * k:8 * k + cap, 0:peers] = field
    by_peer = stage[:, 0:128].T
    rows = 8 * peers
    repeat = (iota((rows, 128), 1) == iota((rows, 128), 0) // 8).astype(F32).astype(BF)
    spread = sum(dot(repeat, part) for part in split3(by_peer))
    spread = jnp.where(iota((rows, 128), 0) % 8 == iota((rows, 128), 1) % 8, spread, 0.0)
    collect = (iota((128, 128), 0) // 8 == iota((128, 128), 1)).astype(F32).astype(BF)
    meta_out[...] = sum(dot(part, collect) for part in split3(spread))


def learner_kernel(
    sizes,
    x_in, act, game, ret, boot, weight, index, count, table, legal, w1, w2, w3, r1, r2, r3, r4, rv, ra, value, advantage,
    dense_in,
    dg_out, sp_out, lp_out, q_out, tab_out,
    x_buf, x3, a1, s1, a2, s2, a3, s3, g3, g2, dw, t1, t2a, t2b, t2c, t3a, t3b, u2, u3, acc,
    bias, stage, pack, head_w, legal_t, meta_out, meta_in, q_send, q_in, a3t, a_in, g4_send, g4_in,
    part, codes, z_in, dg, sp, sp_in, sp_mid, sp_z, sp_all, lp, lp_in, lp_mid, lp_z, lp_all,
    x_sem, dw_sem, out_sem, leave_sem, join_sem, act_sem, act_core_sem, z_sem, near_sem, diag_sem,
):
    hsize, dsize, zrows = sizes
    zsize = dsize // 2
    peers = hsize * dsize
    region = sum(zrows) * (zsize // 2)
    group, share = small_group(sizes)
    h = lax.axis_index("hst")
    d = lax.axis_index("dev")
    z = d // 2
    core = d % 2
    mine = 2 * h + core
    me = h * dsize + d

    def where_is(peer):
        return (peer // dsize, peer % dsize)

    arrive = {
        "act": act_sem, "act_core": act_core_sem, "gather_z": z_sem, "gather_near": near_sem, "gather_diag": diag_sem,
    }

    def transfer(kind, at, src, dst, device):
        leave = leave_sem.at[LEAVE.index(kind if kind in LEAVE else kind + str(at[0]))]
        if kind in arrive:
            join = arrive[kind].at[at]
        else:
            join = join_sem.at[JOIN.index(kind if kind in JOIN else kind + str(at[0]))]
        return pltpu.make_async_remote_copy(
            src_ref=src, dst_ref=dst, send_sem=leave, recv_sem=join, device_id=device, device_id_type=MESH
        )

    def send(kind, at, src, dst, device):
        transfer(kind, at, src, dst, device).start()

    def landed(kind, at, dst):
        transfer(kind, at, dst, dst, (h, d)).wait_recv()

    def sent(kind, at, src):
        transfer(kind, at, src, src, (h, d)).wait_send()

    def fetch(c, slot, count=PIXELS):
        return pltpu.make_async_copy(
            x_in.at[pl.ds(pl.multiple_of(PIXELS * c, 16), count)], x_buf.at[slot, pl.ds(0, count)], x_sem.at[slot]
        )

    last = h >= 0

    @pl.when(last)
    def _():
        for c in range(SLOTS):
            fetch(c, c).start()
        barrier = pltpu.get_barrier_semaphore()

        def greet(k, carry):
            pl.semaphore_signal(barrier, inc=1, device_id=where_is((me + k) % peers), device_id_type=MESH)
            return carry

        lax.fori_loop(1, peers, greet, 0)
        pltpu.make_async_copy(dense_in, dw.at[pl.ds(0, FLAT)], dw_sem).start()
        dw[pl.ds(FLAT, 64)] = jnp.zeros((64, HIDDEN), BF)
        build_toeplitz(w1, w2, w3, t1, t2a, t2b, t2c, t3a, t3b)

    @pl.when(last)
    def _():
        expand_bias((r1, r2, r3, r4, rv, ra), stage, pack, bias)
        prepare_heads(value, advantage, legal, stage, head_w, legal_t)
        prepare_meta(act, game, ret, boot, weight, index, count, stage, meta_out)

    def chunk(c, carry):
        slot = c % SLOTS
        fetch(c, slot).wait()
        relayout(x_buf.at[slot], x3, 8 * c + 4)

        @pl.when(c + SLOTS < CHUNKS - 1)
        def _():
            fetch(c + SLOTS, slot).start()

        @pl.when(c + SLOTS == CHUNKS - 1)
        def _():
            fetch(CHUNKS - 1, slot, PIXELS // 2).start()

        conv1_rows(c, x3, t1, bias, a1, s1)
        return carry

    lax.fori_loop(0, 4, chunk, 0)

    @pl.when(last)
    def _():
        pl.semaphore_wait(pltpu.get_barrier_semaphore(), peers - 1)

        def give(k, carry):
            peer = (me + k) % peers
            send(
                "meta", k, meta_out.at[pl.ds(pl.multiple_of(8 * peer, 8), 8)],
                meta_in.at[pl.ds(pl.multiple_of(8 * me, 8), 8)], where_is(peer),
            )
            return carry

        lax.fori_loop(1, peers, give, 0)

    lax.fori_loop(4, CHUNKS - 1, chunk, 0)

    @pl.when(last)
    def _():
        slot = (CHUNKS - 1) % SLOTS
        fetch(CHUNKS - 1, slot, PIXELS // 2).wait()
        relayout(x_buf.at[slot], x3, 8 * (CHUNKS - 1) + 4, 4)
        conv1_rows(CHUNKS - 1, x3, t1, bias, a1, s1, (0,))

    sibling = (h, 2 * z + 1 - core)
    row_me = pl.ds(pl.multiple_of(8 * me, 8), 8)
    hy, hx = h // 2, h % 2
    flip_x, flip_y = 2 * hy + 1 - hx, 2 * (1 - hy) + hx
    near = (1 - core) * flip_x + core * flip_y
    far = (1 - core) * flip_y + core * flip_x
    across = 3 - h

    def plane(j):
        return (j // 2, 2 * z + j % 2)

    def features(f, to):
        return a3t.at[pl.ds(pl.multiple_of(784 * to + START[f], 16), ROWS[f])]

    def received(f, src):
        return a_in.at[src, pl.ds(ROWS[0] * f, ROWS[f])]

    def send_features(f):
        for k in range(1, hsize):
            to = (h + k) % hsize
            send("act", (f, k), features(f, to), received(f, mine), (to, d))
        send("act_core", (f, 0), features(f, h), received(f, mine), sibling)

    def forward_features(f):
        for k in range(1, hsize):
            src = 2 * ((h - k + hsize) % hsize) + core
            landed("act", (f, k), received(f, src))
            send("act_core", (f, k), received(f, src), received(f, src), sibling)

    def partial(f):
        for k in range(hsize):
            src = 2 * ((h - k + hsize) % hsize) + 1 - core
            landed("act_core", (f, k), received(f, src))
        if f == 0:
            landed("g4", 0, g4_in.at[pl.ds(0, 2 * hsize - 1)])
        left = jnp.concatenate([received(f, j)[...] for j in range(2 * hsize)], 1)
        right = jnp.concatenate([g4_in[j] for j in range(2 * hsize)], 0)
        product = dot(left, right)
        n = zrows[f]
        spare = jnp.zeros((n * (zsize // 2) - ROWS[f], 128), F32)
        for lanes in range(2):
            column = product[:, 128 * lanes:128 * lanes + 128]
            if spare.shape[0]:
                column = jnp.concatenate([column, spare], 0)
            for j in range(zsize // 2):
                chunk = column[n * j:n * j + n]
                part[f, 2 * j + lanes, 0:n] = chunk
                codes[f, 2 * j + lanes, 0:n], codes[f, 2 * j + lanes, n:n + 16] = to_fixed(chunk)
        for k in range(1, zsize):
            to = (z + k) % zsize
            send("sum", (f, k), codes.at[f, to, pl.ds(0, n + 16)], z_in.at[f, z, pl.ds(0, n + 16)], (h, 2 * to + core))

    def corner(f, hh, zz, cc):
        rows = region * hh + zrows[0] * (zsize // 2) * f + zrows[f] * (zz // 2)
        return pl.multiple_of(rows, 16), pl.multiple_of(256 * cc + 128 * (zz % 2), 128)

    def place(f, hh, zz, cc):
        rows, lanes = corner(f, hh, zz, cc)
        return dg.at[pl.ds(rows, zrows[f]), pl.ds(lanes, 128)]

    def spread(f, zz, k):
        at = place(f, h, zz, core)
        send("gather_near", (f, 0, k), at, at, (near, d))
        send("gather_near", (f, 1, k), at, at, (far, d))
        send("gather_core", (f, 0, k), at, at, sibling)

    def finish(f):
        n = zrows[f]
        landed("sum", (f, 0), z_in.at[f, pl.ds(0, zsize - 1), pl.ds(0, n + 16)])
        total = part[f, z, 0:n]
        for k in range(1, zsize):
            src = (z - k + zsize) % zsize
            total = total + from_fixed(z_in[f, src, 0:n], z_in[f, src, n:n + 16])
        rows, lanes = corner(f, h, z, core)
        dg[pl.ds(rows, n), pl.ds(lanes, 128)] = total.astype(BF)
        at = place(f, h, z, core)
        for k in range(1, zsize):
            send("gather_z", (f, k), at, at, (h, 2 * ((z + k) % zsize) + core))
        spread(f, z, 0)

    def pass_on(f):
        for k in range(1, zsize):
            zz = (z - k + zsize) % zsize
            landed("gather_z", (f, k), place(f, h, zz, core))
            spread(f, zz, k)

    def pass_across(f, first=0, count=99):
        for k in range(first, min(first + count, zsize)):
            zz = (z - k + zsize) % zsize
            at = place(f, near, zz, core)
            landed("gather_near", (f, 0, k), at)
            send("gather_diag", (f, k), at, at, (far, d))
            send("gather_core", (f, 1, k), at, at, sibling)
            at = place(f, far, zz, core)
            landed("gather_near", (f, 1, k), at)
            send("gather_core", (f, 2, k), at, at, sibling)

    def pass_last(f):
        for k in range(zsize):
            at = place(f, across, (z - k + zsize) % zsize, core)
            landed("gather_diag", (f, k), at)
            send("gather_core", (f, 3, k), at, at, sibling)

    def gather_core(f):
        landed("gather_core", (f, 0), dg.at[pl.ds(0, zrows[f] * zsize)])

    def group_rows(j):
        return pl.ds(pl.multiple_of(group * j, 8), group)

    def share_rows(j, zz):
        return pl.ds(pl.multiple_of(group * j + share * zz, 8), share)

    def small_send():
        for k in range(1, 2 * hsize):
            to = (mine + k) % (2 * hsize)
            send("small", k, sp.at[group_rows(to)], sp_in.at[mine], plane(to))
        sp_in[mine] = sp[group_rows(mine), :]

    def small_sum():
        landed("small", 0, sp_in.at[pl.ds(0, 2 * hsize - 1)])
        total = sp_in[0]
        for j in range(1, 2 * hsize):
            total = total + sp_in[j]
        sp_mid[...] = total
        for k in range(1, zsize):
            to = (z + k) % zsize
            send("small_z", k, sp_mid.at[pl.ds(pl.multiple_of(share * to, 8), share)], sp_z.at[z], (h, 2 * to + core))
        sp_z[z] = sp_mid[pl.ds(pl.multiple_of(share * z, 8), share), :]

    def small_finish():
        landed("small_z", 0, sp_z.at[pl.ds(0, zsize - 1)])
        total = sp_z[0]
        for j in range(1, zsize):
            total = total + sp_z[j]
        sp_all[share_rows(mine, z), :] = total
        at = sp_all.at[share_rows(mine, z)]
        for k in range(1, zsize):
            send("small_back", k, at, at, (h, 2 * ((z + k) % zsize) + core))

    def small_spread():
        landed("small_back", 0, sp_z.at[pl.ds(0, zsize - 1)])
        at = sp_all.at[group_rows(mine)]
        for k in range(1, hsize):
            send("small_all", k, at, at, ((h + k) % hsize, d))
        send("small_core", 0, at, at, sibling)

    def small_share():
        landed("small_all", 0, sp_in.at[pl.ds(0, hsize - 1)])
        for k in range(1, hsize):
            at = sp_all.at[group_rows(2 * ((h - k + hsize) % hsize) + core)]
            send("small_core", k, at, at, sibling)

    def late_rows(j):
        return pl.ds(pl.multiple_of(16 * j, 16), 16)

    def late_send():
        for k in range(1, 2 * hsize):
            to = (mine + k) % (2 * hsize)
            send("late", k, lp.at[late_rows(to)], lp_in.at[mine], plane(to))
        lp_in[mine] = lp[late_rows(mine), :]

    def late_sum():
        landed("late", 0, lp_in.at[pl.ds(0, 2 * hsize - 1)])
        total = lp_in[0]
        for j in range(1, 2 * hsize):
            total = total + lp_in[j]
        lp_mid[...] = total
        lp_z[z] = total
        for k in range(1, zsize):
            send("late_z", k, lp_mid, lp_z.at[z], (h, 2 * ((z + k) % zsize) + core))

    def late_spread():
        landed("late_z", 0, lp_z.at[pl.ds(0, zsize - 1)])
        total = lp_z[0]
        for j in range(1, zsize):
            total = total + lp_z[j]
        lp_all[late_rows(mine), :] = total
        at = lp_all.at[late_rows(mine)]
        for k in range(1, 2 * hsize):
            send("late_all", k, at, at, plane((mine + k) % (2 * hsize)))

    def dense_out(f):
        first, count = zrows[0] * (zsize // 2) * f, zrows[f] * (zsize // 2)
        return [
            pltpu.make_async_copy(
                dg.at[pl.ds(region * j + first, count)], dg_out.at[pl.ds(region * j + first, count)],
                out_sem.at[hsize * f + j],
            )
            for j in range(hsize)
        ]

    @pl.when(last)
    def _():
        conv2_all(a1, t2a, t2b, t2c, bias, a2, s2)
        conv3_all(a2, t3a, t3b, bias, a3, s3)
        for r in range(7):
            a3t[pl.ds(448 * r, 448), :] = a3[r].T[0:448]
        send_features(0)

    @pl.when(last)
    def _():
        pltpu.make_async_copy(dense_in, dw.at[pl.ds(0, FLAT)], dw_sem).wait()
        act4, slope4, head = dense_head(a3, dw, head_w, bias)

        landed("meta", 0, meta_in.at[pl.ds(0, 8 * (peers - 1))])
        meta_in[row_me, :] = meta_out[row_me, :]
        q, grow, dhb, loss, newt, top = td_part(
            head, meta_in[...], meta_out[...], legal_t[...], table[...], 8 * peers, float(peers * act.shape[0])
        )
        g4, dhw = head_grads(grow, act4, slope4, head_w)
        for half in range(2):
            g4_send[half] = g4[:, 256 * half:256 * half + 256]
        for k in range(1, 2 * hsize):
            to = (mine + k) % (2 * hsize)
            send("g4", k, g4_send.at[to % 2], g4_in.at[mine], plane(to))
        send_features(1)
        g4_in[mine] = g4_send[core]
        for f in range(2):
            received(f, mine)[...] = features(f, h)[...]
        tab_out[...] = jnp.broadcast_to(newt, (8, 128))
        lane = iota((8 * peers, 128), 1)
        q_send[...] = jnp.where(lane == 19, top, jnp.where(lane == 20, loss, q))
        for k in range(4):
            sp[pl.ds(640 + 24 * k, 24), :] = dhw[0:24, 128 * k:128 * k + 128]
        b4 = jnp.sum(g4.astype(F32), 0, keepdims=True)
        for k in range(4):
            sp[738 + k:739 + k, :] = b4[:, 128 * k:128 * k + 128]
        sp[742:743, :] = dhb
        sp[743:2 * hsize * group, :] = jnp.zeros((2 * hsize * group - 743, 128), F32)
        lp[64:, :] = jnp.zeros((lp.shape[0] - 64, 128), F32)
        sp[737:738, :] = fold64(g3_all(g4, dw, s3, g3))

    @pl.when(last)
    def _():
        build_transposed(w2, w3, u2, u3)

    @pl.when(last)
    def _():
        sp[736:737, :] = fold64(conv3_dx(g3, u3, s2, g2))
        forward_features(0)

    @pl.when(last)
    def _():
        conv3_dw(a2, g3, sp, 256)

    @pl.when(last)
    def _():
        conv2_dw(a1, g2, sp, 0, 0, 4)

    @pl.when(last)
    def _():
        partial(0)
        small_send()

    @pl.when(last)
    def _():
        stage[0:1, 0:256] = conv2_dx(g2, u2, s1, a1, 0, 2)
        forward_features(1)

    @pl.when(last)
    def _():
        b1 = conv2_dx(g2, u2, s1, a1, 2, 4) + stage[0:1, 0:256]
        b1 = b1[:, 0:128] + b1[:, 128:256]
        b1 = b1 + pltpu.roll(b1, 64, 1)
        lp[64:65, :] = b1 + pltpu.roll(b1, 32, 1)

    @pl.when(last)
    def _():
        partial(1)

    @pl.when(last)
    def _():
        conv1_dw(x3, a1, acc, 0, 2)

    @pl.when(last)
    def _():
        small_sum()
        finish(0)

    @pl.when(last)
    def _():
        conv1_dw(x3, a1, acc, 2, 5)

    @pl.when(last)
    def _():
        conv1_fold(acc, lp, 0)
        late_send()
        small_finish()
        pass_on(0)
        finish(1)
        late_sum()
        small_spread()
        pass_across(0)
        pass_on(1)

        def answer(k, carry):
            peer = (me + k) % peers
            send(
                "q", k, q_send.at[pl.ds(pl.multiple_of(8 * peer, 8), 8)],
                q_in.at[pl.ds(pl.multiple_of(8 * me, 8), 8)], where_is(peer),
            )
            return carry

        lax.fori_loop(1, peers, answer, 0)
        q_in[row_me, :] = q_send[row_me, :]

        pass_last(0)
        pass_across(1, 0, 2)
        late_spread()
        gather_core(0)
        first_half = dense_out(0)
        for copy in first_half:
            copy.start()
        pass_across(1, 2, zsize)
        small_share()
        pass_last(1)
        landed("small_core", 0, sp_in.at[pl.ds(0, hsize)])
        landed("late_all", 0, lp_in.at[pl.ds(0, 2 * hsize - 1)])

        landed("q", 0, q_in.at[pl.ds(0, 8 * (peers - 1))])
        others = [
            pltpu.make_async_copy(src, dst, out_sem.at[2 * hsize + k])
            for k, (src, dst) in enumerate(((sp_all, sp_out), (lp_all, lp_out), (q_in, q_out)))
        ]
        for copy in others:
            copy.start()
        gather_core(1)
        second_half = dense_out(1)
        for copy in second_half:
            copy.start()

        sent("meta", 0, meta_in.at[pl.ds(0, 8 * (peers - 1))])
        sent("q", 0, q_in.at[pl.ds(0, 8 * (peers - 1))])
        sent("act", (0, 0), a_in.at[pl.ds(0, hsize - 1)])
        sent("act_core", (0, 0), a_in.at[pl.ds(0, hsize)])
        sent("g4", 0, g4_in.at[pl.ds(0, 2 * hsize - 1)])
        sent("small", 0, sp_in.at[pl.ds(0, 2 * hsize - 1)])
        sent("small_z", 0, sp_z.at[pl.ds(0, zsize - 1)])
        sent("small_back", 0, sp_z.at[pl.ds(0, zsize - 1)])
        sent("small_all", 0, sp_in.at[pl.ds(0, hsize - 1)])
        sent("small_core", 0, sp_in.at[pl.ds(0, hsize)])
        sent("late", 0, lp_in.at[pl.ds(0, 2 * hsize - 1)])
        sent("late_z", 0, lp_z.at[pl.ds(0, zsize - 1)])
        sent("late_all", 0, lp_in.at[pl.ds(0, 2 * hsize - 1)])
        for f in range(2):
            n = zrows[f]
            sent("sum", (f, 0), z_in.at[f, pl.ds(0, zsize - 1), pl.ds(0, n + 16)])
            sent("gather_z", (f, 0), dg.at[pl.ds(0, n * (zsize - 1)), pl.ds(0, 128)])
            sent("gather_near", (f, 0, 0), dg.at[pl.ds(0, n * zsize), pl.ds(0, 256)])
            sent("gather_diag", (f, 0), dg.at[pl.ds(0, n * zsize), pl.ds(0, 128)])
            sent("gather_core", (f, 0), dg.at[pl.ds(0, n * zsize)])
        for copy in first_half + others + second_half:
            copy.wait()


def small_group(sizes):
    hsize, dsize, _ = sizes
    zsize = dsize // 2
    group = -(-743 // (2 * hsize * 8 * zsize)) * 8 * zsize
    return group, group // zsize


def learner(sizes, args, cap):
    hsize, dsize, zrows = sizes
    zsize, peers = dsize // 2, hsize * dsize
    region = sum(zrows) * (zsize // 2)
    group, share = small_group(sizes)
    dma = pltpu.SemaphoreType.DMA
    vmem = pltpu.VMEM
    groups = 2 * hsize
    scratch = [
        vmem((SLOTS, PIXELS, 128), BF), vmem((88, 128, 384), BF), vmem((21, 128, 768), BF), vmem((21, 128, 768), F32), vmem((9, 128, 640), BF),
        vmem((9, 128, 640), F32), vmem((7, 128, 512), BF), vmem((7, 128, 512), F32), vmem((11, 128, 512), BF),
        vmem((11, 128, 640), BF), vmem((3200, 512), BF), vmem((1024, 256), BF), vmem((2048, 256), BF),
        vmem((2048, 256), BF), vmem((1024, 128), BF), vmem((1536, 256), BF), vmem((1152, 256), BF),
        vmem((2, 2304, 256), BF), vmem((3072, 256), BF), vmem((256, 1024), F32),
        vmem((1, 2048), F32), vmem((128, 512), F32), vmem((8, 128), BF), vmem((128, 512), BF), vmem((128, 128), BF),
        vmem((8 * peers, 128), F32), vmem((8 * peers, 128), F32), vmem((8 * peers, 128), F32),
        vmem((8 * peers, 128), F32), vmem((FLAT, 128), BF), vmem((groups, sum(ROWS), 128), BF), vmem((2, 128, 256), BF),
        vmem((groups, 128, 256), BF), vmem((2, zsize, max(zrows), 128), F32), vmem((2, zsize, max(zrows) + 16, 128), jnp.int16),
        vmem((2, zsize, max(zrows) + 16, 128), jnp.int16), vmem((hsize * region, 512), BF),
        vmem((groups * group, 128), F32), vmem((groups, group, 128), F32), vmem((group, 128), F32),
        vmem((zsize, share, 128), F32), vmem((groups * group, 128), F32),
        vmem((16 * groups, 128), F32), vmem((groups, 16, 128), F32), vmem((16, 128), F32), vmem((zsize, 16, 128), F32),
        vmem((16 * groups, 128), F32),
        dma((SLOTS,)), dma, dma((2 * hsize + 3,)), dma((len(LEAVE),)), dma((len(JOIN),)),
        dma((2, hsize)), dma((2, hsize)), dma((2, zsize)), dma((2, 2, zsize)), dma((2, zsize)),
    ]
    whole = pl.BlockSpec(memory_space=pltpu.VMEM)
    outside = pl.BlockSpec(memory_space=pl.ANY)
    return pl.pallas_call(
        functools.partial(learner_kernel, sizes),
        in_specs=[outside] + [whole] * 20 + [outside],
        out_specs=[outside, outside, outside, outside, whole],
        out_shape=[
            jax.ShapeDtypeStruct((hsize * region, 512), BF),
            jax.ShapeDtypeStruct((groups * group, 128), F32),
            jax.ShapeDtypeStruct((16 * groups, 128), F32),
            jax.ShapeDtypeStruct((8 * peers, 128), F32),
            jax.ShapeDtypeStruct((8, 128), F32),
        ],
        scratch_shapes=scratch,
        compiler_params=pltpu.CompilerParams(collective_id=0, has_side_effects=True, vmem_limit_bytes=63 << 20),
    )(*args)


def output_kernel(
    hsize, region, second, dg, sp, lp, q, tab,
    dense, c1, c2, c3, bias1, bias2, bias3, bias4, vw, vb, aw, ab, loss, top, table, qt,
    held, wide, in_sem, out_sem,
):
    reads = []
    for j in range(2 * hsize):
        f = j % 2
        src, at, count = region * (j // 2) + f * (second + 16), 784 * (j // 2) + f * ROWS[0], ROWS[f] - 16 * f
        copy = pltpu.make_async_copy(dg.at[pl.ds(src, count)], held.at[pl.ds(at, count)], in_sem.at[j])
        reads.append((copy, at, count))
    for copy, _, _ in reads:
        copy.start()
    for a in range(2):
        c1[pl.ds(128 * a, 128), :] = lp[pl.ds(32 * a, 32), :].T
    for kr in range(4):
        c2[pl.ds(128 * kr, 128), :] = sp[pl.ds(64 * kr, 64), :].T
    for kr in range(3):
        c3[pl.ds(192 * kr, 128), :] = sp[pl.ds(256 + 128 * kr, 64), :].T
        c3[pl.ds(192 * kr + 128, 64), :] = sp[pl.ds(320 + 128 * kr, 64), :].T[0:64]
    bias1[...] = lp[64:65, 0:32]
    bias2[...] = sp[736:737, 0:64]
    bias3[...] = sp[737:738, 0:64]
    for k in range(4):
        bias4[:, 128 * k:128 * k + 128] = sp[738 + k:739 + k, :]
        heads = sp[pl.ds(640 + 24 * k, 24), :]
        aw[:, 128 * k:128 * k + 128] = heads[0:ACTIONS]
        vw[:, 128 * k:128 * k + 128] = heads[ACTIONS:ACTIONS + 1]
    ab[...] = sp[742:743, 0:ACTIONS]
    vb[...] = sp[742:743, ACTIONS:ACTIONS + 1]
    rows = q[...]
    top[...] = jnp.max(rows[:, 19:20], 0, keepdims=True)
    first = iota((rows.shape[0], 1), 0) % 8 == 0
    loss[...] = jnp.sum(jnp.where(first, rows[:, 20:21], 0.0), 0, keepdims=True)
    table[...] = tab[0:1, :]
    turned = rows.T
    for k in range(ACTIONS):
        qt[k] = turned[k:k + 1]
    writes = []
    for j, (copy, at, count) in enumerate(reads):
        copy.wait()
        wide[pl.ds(at, count)] = held[pl.ds(at, count)].astype(F32)
        writes.append(pltpu.make_async_copy(wide.at[pl.ds(at, count)], dense.at[pl.ds(at, count)], out_sem.at[j]))
        writes[-1].start()
    for copy in writes:
        copy.wait()


def outputs(sizes, dg, sp, lp, q, tab):
    hsize, dsize, zrows = sizes
    region, second = sum(zrows) * (dsize // 4), zrows[0] * (dsize // 4)
    whole = pl.BlockSpec(memory_space=pltpu.VMEM)
    outside = pl.BlockSpec(memory_space=pl.ANY)
    shapes = (
        (FLAT, 512), (256, 32), (512, 64), (576, 64), (1, 32), (1, 64), (1, 64), (1, 512), (1, 512), (1, 1),
        (ACTIONS, 512), (1, ACTIONS), (1, 1), (1, 1), (1, 128), (ACTIONS, 1, 8 * hsize * dsize),
    )
    return pl.pallas_call(
        functools.partial(output_kernel, hsize, region, second),
        in_specs=[outside, whole, whole, whole, whole],
        out_specs=[outside] + [whole] * 15,
        out_shape=[jax.ShapeDtypeStruct(s, F32) for s in shapes],
        scratch_shapes=[
            pltpu.VMEM((FLAT, 512), BF), pltpu.VMEM((FLAT, 512), F32),
            pltpu.SemaphoreType.DMA((2 * hsize,)), pltpu.SemaphoreType.DMA((2 * hsize,)),
        ],
        compiler_params=pltpu.CompilerParams(vmem_limit_bytes=63 << 20),
    )(dg, sp, lp, q, tab)


def per_device(
    hsize,
    dsize,
    replay,
    send_index,
    send_count,
    actions,
    game_ids,
    legal_table,
    returns,
    bootstrap,
    is_weights,
    priority_table,
    conv1_w,
    conv1_b,
    conv2_w,
    conv2_b,
    conv3_w,
    conv3_b,
    dense_w,
    dense_b,
    value_w,
    value_b,
    advantage_w,
    advantage_b,
):
    cap = send_index.shape[2]
    peers = hsize * dsize
    zsize = dsize // 2
    zrows = tuple(-(-rows // (8 * zsize)) * 16 for rows in ROWS)
    sizes = (hsize, dsize, zrows)
    args = (
        replay.T,
        actions[0].T,
        game_ids[0].T,
        returns[0].T,
        bootstrap[0].T,
        is_weights[0].T,
        send_index[0].T,
        send_count,
        priority_table.reshape(1, -1),
        legal_table.T,
        conv1_w.reshape(256, 32),
        conv2_w.reshape(512, 64),
        conv3_w.reshape(576, 64),
        conv1_b.reshape(1, -1),
        conv2_b.reshape(1, -1),
        conv3_b.reshape(1, -1),
        dense_b.reshape(4, -1),
        value_b.reshape(1, -1),
        advantage_b.reshape(1, -1),
        value_w.T,
        advantage_w.T,
        dense_w,
    )
    dg, sp, lp, q, tab = learner(sizes, args, cap)
    (dense, c1, c2, c3, b1, b2, b3, b4, vw, vb, aw, ab, loss, top, table, qt) = outputs(sizes, dg, sp, lp, q, tab)
    q_values = qt.transpose(1, 2, 0)
    if cap != 8:
        q_values = q_values.reshape(1, peers, 8, ACTIONS)[:, :, :cap].reshape(1, peers * cap, ACTIONS)
    return (
        q_values,
        loss.reshape(()),
        c1.reshape(conv1_w.shape),
        b1.reshape(-1),
        c2.reshape(conv2_w.shape),
        b2.reshape(-1),
        c3.reshape(conv3_w.shape),
        b3.reshape(-1),
        dense,
        b4.reshape(-1),
        vw.T,
        vb.reshape(-1),
        aw.T,
        ab.reshape(-1),
        table.reshape(-1),
        top.reshape(()),
    )


def solution(mesh):
    both = ("hst", "dev")
    rows2, rows3 = P(both, None), P(both, None, None)
    placed = (rows2, rows3, rows2, rows3, rows3, P(), rows3, rows3, rows3, P(both)) + (P(),) * 12
    return jax.shard_map(
        functools.partial(per_device, mesh.shape["hst"], mesh.shape["dev"]),
        mesh=mesh,
        in_specs=placed,
        out_specs=(rows3,) + (P(),) * 13 + (P(both), P()),
        check_vma=False,
    )
```

```python
import functools

import jax
import jax.numpy as jnp
from jax import lax
from jax.experimental import pallas as pl
from jax.experimental.pallas import tpu as pltpu
from jax.sharding import PartitionSpec as P

GAMMA_THREE = 0.970299
ACTIONS = 18
FLAT = 3136
HIDDEN = 512
CHUNKS = 11
PIXELS = 2688
SLOTS = 4
MESH = pl.DeviceIdType.MESH
JOIN = (
    "meta", "q", "g4", "sum0", "sum1", "gather_core0", "gather_core1", "small", "small_z", "small_back", "small_all",
    "small_core", "late", "late_z", "late_all",
)
LEAVE = JOIN + (
    "act", "act_core", "gather_z0", "gather_z1", "gather_near0", "gather_near1", "gather_diag0", "gather_diag1",
)
ROWS = (416, 384)
START = (0, 400)
F32=jnp.float32; BF=jnp.bfloat16
NN=(((1,),(0,)),((),())); NT=(((1,),(1,)),((),())); TN=(((0,),(0,)),((),()))

def dot(a,b,dims=NN):
    return lax.dot_general(a,b,dims,preferred_element_type=F32)
def iota(shape,axis): return lax.broadcasted_iota(jnp.int32,shape,axis)
def tile_lanes(w,width,times,keep,dims=NN):
    n=width*times
    e=((iota((width,n),1)%width==iota((width,n),0)) & (iota((width,n),1)<keep*width)).astype(BF)
    return dot(w,e,dims)

def build_toeplitz(w1,w2,w3,t1,t2a,t2b,t2c,t3a,t3b):
    lane32=iota((16,256),1)//32
    wt1=tile_lanes(w1[...],32,8,7)
    for kr in range(8):
        lo=wt1[32*kr:32*kr+16]; hi=wt1[32*kr+16:32*kr+32]
        for b in range(8):
            t1[pl.ds(128*kr+16*b,16),:]=(jnp.where(lane32==b,lo,0.0)+jnp.where(lane32==b-1,hi,0.0)).astype(BF)
    lane64=iota((32,256),1)//64
    wt2=tile_lanes(w2[...],64,4,4)
    def blk2(kr,p,n,cl):
        col=7*p+cl
        out=jnp.zeros((32,256),F32)
        if cl>=(7 if p<2 else 6): return out
        for kc in range(4):
            if (col-kc)%2: continue
            j=(col-kc)//2
            if 0<=j<9 and 4*n<=j<4*n+4:
                out=out+jnp.where(lane64==j-4*n,wt2[(4*kr+kc)*32:(4*kr+kc)*32+32],0.0)
        return out
    for kr in range(4):
        for cl in range(8):
            for ref,pairs in ((t2a,((0,0),(1,0))),(t2b,((1,1),(2,1)))):
                for k,(p,n) in enumerate(pairs):
                    ref[pl.ds(512*kr+256*k+32*cl,32),:]=blk2(kr,p,n,cl).astype(BF)
            t2c[pl.ds(256*kr+32*cl,32),:]=blk2(kr,2,2,cl)[:,:128].astype(BF)
    lane64b=iota((64,256),1)//64
    wt3=tile_lanes(w3[...],64,4,4)
    def blk3(kr,t,m,cl):
        col=4*t+cl
        out=jnp.zeros((64,256),F32)
        if col>8: return out
        for kc in range(3):
            j=col-kc
            if 0<=j<7 and 4*m<=j<4*m+4:
                out=out+jnp.where(lane64b==j-4*m,wt3[(3*kr+kc)*64:(3*kr+kc)*64+64],0.0)
        return out
    for kr in range(3):
        for cl in range(4):
            t3a[pl.ds(512*kr+64*cl,64),:]=blk3(kr,0,0,cl).astype(BF)
            t3a[pl.ds(512*kr+256+64*cl,64),:]=blk3(kr,1,0,cl).astype(BF)
            t3b[pl.ds(384*kr+64*cl,64),:]=blk3(kr,1,1,cl).astype(BF)
            if cl<2:
                t3b[pl.ds(384*kr+256+64*cl,64),:]=blk3(kr,2,1,cl).astype(BF)

def build_transposed(w2,w3,u2,u3):
    lane64b=iota((64,256),1)//64
    lane32c=iota((64,256),1)//32
    wx2=[[tile_lanes(w2[pl.ds((4*kr+kc)*32,32),:],32,8,8,TN) for kc in range(4)] for kr in range(4)]
    def ublk2(kr,p,j):
        out=jnp.zeros((64,256),F32)
        if j>8: return out
        for kc in range(4):
            cl=2*j+kc-7*p
            if 0<=cl<(7 if p<2 else 6):
                out=out+jnp.where(lane32c==cl,wx2[kr][kc],0.0)
        return out
    for par in range(2):
        for k2 in range(2):
            kr=par+2*k2
            for jl in range(4):
                u2[par,pl.ds(256*k2+64*jl,64),:]=ublk2(kr,0,jl).astype(BF)
            for j in range(8):
                u2[par,pl.ds(512+512*k2+64*j,64),:]=ublk2(kr,1,j).astype(BF)
            for jl in range(6):
                u2[par,pl.ds(1536+384*k2+64*jl,64),:]=ublk2(kr,2,4+jl).astype(BF)
    wx3=[[tile_lanes(w3[pl.ds((3*kr+kc)*64,64),:],64,4,4,TN) for kc in range(3)] for kr in range(3)]
    def ublk3(kr,t,j):
        out=jnp.zeros((64,256),F32)
        if j>6: return out
        for kc in range(3):
            cl=j+kc-4*t
            if 0<=cl<4 and j+kc<=8:
                out=out+jnp.where(lane64b==cl,wx3[kr][kc],0.0)
        return out
    for kr in range(3):
        for jl in range(4):
            u3[pl.ds(256*kr+64*jl,64),:]=ublk3(kr,0,jl).astype(BF)
        for j in range(8):
            u3[pl.ds(768+512*kr+64*j,64),:]=ublk3(kr,1,j).astype(BF)
        for jl in range(4):
            u3[pl.ds(2304+256*kr+64*jl,64),:]=ublk3(kr,2,4+jl).astype(BF)

def gates(pre):
    s=1.0/(1.0+jnp.exp(-pre))
    return pre*s, s*(1.0+pre*(1.0-s))

def relayout(x, x3, base, rows=8):
    keep = iota((128, 128), 1) < 112
    for r in range(rows):
        for p in range(3):
            at = r * 336 + 112 * p
            if at + 128 <= 336 * rows:
                v = x[at:at + 128, :]
            else:
                v = jnp.concatenate([x[at:336 * rows, :], jnp.zeros((at + 128 - 336 * rows, 128), BF)], 0)
            v = v.T
            if p == 2:
                v = jnp.where(keep, v, jnp.zeros_like(v))
            x3[base + r, :, 128 * p:128 * p + 128] = v

def conv1_rows(c,x3,t1,bias,a1,s1,which=(0,1)):
    L=[]
    for q in which:
        for p in range(3):
            L.append(jnp.concatenate([x3[8*c+4*q+kr,:,128*p:128*p+128] for kr in range(8)],axis=1))
    pre=dot(jnp.concatenate(L,axis=0),t1[...])+bias[:,0:256]
    act,slope=gates(pre)
    for q in which:
        for p in range(3):
            k=(3*(q-which[0])+p)*128
            a1[2*c+q,:,256*p:256*p+256]=act[k:k+128].astype(BF)
            s1[2*c+q,:,256*p:256*p+256]=slope[k:k+128]

def conv2_all(a1,t2a,t2b,t2c,bias,a2,s2):
    rows=[[a1[2*(q)+kr+1] for kr in range(4)] for q in range(9)]
    def lhs(lo,hi):
        return jnp.concatenate([jnp.concatenate([rows[q][kr][:,lo:hi] for kr in range(4)],1) for q in range(9)],0)
    for (lo,hi,w,o0,o1) in ((0,512,t2a,0,256),(256,768,t2b,256,512),(512,768,t2c,512,640)):
        pre=dot(lhs(lo,hi),w[...])+bias[:,256+o0:256+o1]
        act,slope=gates(pre)
        for q in range(9):
            a2[q,:,o0:o1]=act[128*q:128*q+128].astype(BF)
            s2[q,:,o0:o1]=slope[128*q:128*q+128]

def conv3_all(a2,t3a,t3b,bias,a3,s3):
    for i0,n in ((0,4),(4,3)):
        for lo,hi,w,o0 in ((0,512,t3a,0),(256,640,t3b,256)):
            L=jnp.concatenate([jnp.concatenate([a2[i0+q+kr][:,lo:hi] for kr in range(3)],1) for q in range(n)],0)
            pre=dot(L,w[...])+bias[:,896+o0:896+o0+256]
            act,slope=gates(pre)
            if o0: slope=jnp.where(iota((128*n,256),1)<192,slope,0.0)
            for q in range(n):
                a3[i0+q,:,o0:o0+256]=act[128*q:128*q+128].astype(BF)
                s3[i0+q,:,o0:o0+256]=slope[128*q:128*q+128]

def dense_head(a3,dw,hw,bias):
    pre=bias[:,1408:1920]
    for r in range(7):
        pre=pre+dot(a3[r],dw[pl.ds(448*r,512),:])
    act,slope=gates(pre)
    act4=act.astype(BF)
    head=dot(act4,hw[...],NT)+bias[:,1920:2048]
    return act4,slope,head

def split2(v):
    hi=v.astype(BF); return hi,(v-hi.astype(F32)).astype(BF)
def split3(v):
    hi=v.astype(BF); r=v-hi.astype(F32); mid=r.astype(BF); return hi,mid,(r-mid.astype(F32)).astype(BF)

def td_part(head,meta,local,legal,table,slots,live_slots):
    lane=iota((slots,128),1)
    idx=local[:,4:5].astype(jnp.int32); live=local[:,5:6]
    action=meta[:,0:1].astype(jnp.int32); game=meta[:,1:2].astype(jnp.int32)
    target=meta[:,2:3]; weight=meta[:,3:4]
    pick=lane==idx
    pickb=pick.astype(F32).astype(BF)
    h=None
    for part in split3(head):
        d=dot(pickb,part); h=d if h is None else h+d
    game_pick=(lane==game).astype(F32).astype(BF)
    mask=dot(game_pick,legal,NT)
    counted=jnp.sum(mask,1,keepdims=True)
    centre=jnp.sum(h*mask,1,keepdims=True)/counted
    q=h[:,ACTIONS:ACTIONS+1]+h-centre
    act_pick=(lane==action).astype(F32)
    td=target-jnp.sum(q*act_pick,1,keepdims=True)
    scaled=live*weight
    mag=jnp.abs(td)
    hub=jnp.where(mag<=1.0,0.5*td*td,mag-0.5)
    loss=jnp.sum(scaled*hub,0,keepdims=True)/live_slots
    gt=-scaled*jnp.clip(td,-1.0,1.0)/live_slots
    G=(gt*(act_pick+(lane==ACTIONS).astype(F32))-mask*(gt/counted)).astype(BF)
    pr=live*jnp.exp(0.3*jnp.log(td*td+1.0))
    fresh=jnp.max(jnp.where(pick,pr,0.0),0,keepdims=True)
    newt=jnp.where(fresh>0.0,fresh,table)
    top=jnp.max(newt,1,keepdims=True)
    grow=dot(pickb,G,TN)
    dhb=jnp.sum(G.astype(F32),0,keepdims=True)
    return q,grow,dhb,loss,newt,top

def head_grads(grow,act4,slope4,hw):
    hi,lo=split2(grow)
    up4=dot(hi,hw[...])+dot(lo,hw[...])
    dhw=dot(hi,act4,TN)+dot(lo,act4,TN)
    g4=(up4*slope4).astype(BF)
    return g4,dhw

def g3_all(g4,dw,s3,g3):
    z=jnp.zeros((128,512),BF)
    for r in (0,1,9,10): g3[r]=z
    b3=None
    for r in range(7):
        up=dot(g4,dw[pl.ds(448*r,512),:],NT)
        g=(up*s3[r]).astype(BF)
        g3[r+2]=g
        b=g.astype(F32); b3=b if b3 is None else b3+b
    return jnp.sum(b3,0,keepdims=True)

def fold64(row):
    n=row.shape[1]//128
    t=row[:,0:128]
    for k in range(1,n): t=t+row[:,128*k:128*k+128]
    return t+pltpu.roll(t,64,1)

def conv3_dw(a2,g3,sp,base):
    low=iota((64,128),1)<64
    G=jnp.concatenate([g3[r+2] for r in range(7)],0)
    def lhs(lo,hi):
        return jnp.concatenate([jnp.concatenate([a2[i+kr][:,lo:hi] for kr in range(3)],1) for i in range(7)],0)
    d0=dot(G[:,0:256],lhs(0,512),TN)
    d1=dot(G[:,256:512],lhs(256,640),TN)
    for kr in range(3):
        E0=E1=O0=O1=None
        for j in range(7):
            def T(ct):
                if j<4: return d0[64*j:64*j+64,512*kr+128*ct:512*kr+128*ct+128]
                return d1[64*(j-4):64*(j-4)+64,384*kr+128*(ct-2):384*kr+128*(ct-2)+128]
            add=lambda a,b: b if a is None else a+b
            if j%2==0:
                E0=add(E0,T(j//2)); E1=add(E1,T(j//2+1))
            else:
                O0=add(O0,T(j//2)); O1=add(O1,T(j//2+1))
        o0=pltpu.roll(O0,64,1); o1=pltpu.roll(O1,64,1)
        sp[pl.ds(base+128*kr,64),:]=E0+jnp.where(low,o0,o1)
        sp[pl.ds(base+128*kr+64,64),:]=E1+o1

def conv3_dx(g3,u3,s2,g2):
    z=jnp.zeros((128,640),BF)
    g2[0]=z; g2[10]=z
    def step(s,tot):
        rows=[[g3[3*s+q+2-kr] for kr in range(3)] for q in range(3)]
        def lhs(lo,hi):
            return jnp.concatenate([jnp.concatenate([rows[q][kr][:,lo:hi] for kr in range(3)],1) for q in range(3)],0)
        outs=[]
        for (lo,hi,k0,k1,o0,o1) in ((0,256,0,768,0,256),(0,512,768,2304,256,512),(256,512,2304,3072,512,640)):
            up=dot(lhs(lo,hi),u3[pl.ds(k0,k1-k0),0:o1-o0])
            acc=None
            for q in range(3):
                g=(up[128*q:128*q+128]*s2[3*s+q,:,o0:o1]).astype(BF)
                g2[3*s+q+1,:,o0:o1]=g
                f=g.astype(F32); acc=f if acc is None else acc+f
            outs.append(jnp.sum(acc,0,keepdims=True))
        return tot+jnp.concatenate(outs,1)
    return lax.fori_loop(0,3,step,jnp.zeros((1,640),F32))

def conv2_dw(a1,g2,sp,base,first,last):
    lane=iota((64,128),1)//32
    G=jnp.concatenate([g2[i+1] for i in range(9)],0)
    for kr in range(first,last):
        L=jnp.concatenate([a1[2*i+kr+1] for i in range(9)],0)
        d=[dot(G[:,0:256],L[:,0:512],TN),dot(G[:,256:512],L[:,256:768],TN),dot(G[:,512:640],L[:,512:768],TN)]
        lo=[0,1,2]
        tot=jnp.zeros((64,128),F32)
        for j in range(9):
            n=j//4
            kc=0
            while kc<4:
                col=2*j+kc; p=min(col//7,2); cl=col-7*p
                lim=7 if p<2 else 6
                cnt=min(4-kc,lim-cl)
                v=d[n][64*(j-4*n):64*(j-4*n)+64,256*(p-lo[n]):256*(p-lo[n])+256]
                sh=(32*(kc-cl))%256
                if sh: v=pltpu.roll(v,sh,1)
                v=v[:,0:128]
                tot=tot+(v if cnt==4 else jnp.where((lane>=kc)&(lane<kc+cnt),v,0.0))
                kc+=cnt
        sp[pl.ds(base+64*kr,64),:]=tot

def conv2_dx(g2,u2,s1,g1,first,last):
    def step(t,tot):
        a0=5*(t//2); par=t%2
        def lhs(lo,hi):
            return jnp.concatenate([jnp.concatenate([g2[a0+q+1][:,lo:hi],g2[a0+q][:,lo:hi]],1) for q in range(5)],0)
        outs=[]
        for p,(lo,hi,k0,k1) in enumerate(((0,256,0,512),(0,512,512,1536),(256,640,1536,2304))):
            up=dot(lhs(lo,hi),u2[par,pl.ds(k0,k1-k0),:])
            acc=None
            for q in range(5):
                r=2*(a0+q)+par
                g=(up[128*q:128*q+128]*s1[r+1,:,256*p:256*p+256]).astype(BF)
                g1[r+1,:,256*p:256*p+256]=g
                f=g.astype(F32); acc=f if acc is None else acc+f
            outs.append(jnp.sum(acc,0,keepdims=True))
        return tot+outs[0]+outs[1]+outs[2]
    return lax.fori_loop(first,last,step,jnp.zeros((1,256),F32))

def conv1_dw(x3,g1,acc,first,last):
    if first==0: acc[...]=jnp.zeros_like(acc)
    def step(s,_):
        Ls=[];Gs=[]
        for q in range(4):
            for p in range(3):
                Gs.append(g1[4*s+q+1,:,256*p:256*p+256])
                Ls.append(jnp.concatenate([x3[4*(4*s+q)+kr+4,:,128*p:128*p+128] for kr in range(8)],axis=1))
        acc[...]+=dot(jnp.concatenate(Gs,0),jnp.concatenate(Ls,0),TN)
        return 0
    lax.fori_loop(first,last,step,0)

def conv1_fold(acc,sp,base):
    lane=iota((32,128),1)//32
    for a in range(2):
        out=jnp.zeros((32,128),F32)
        for qq in range(4):
            kr=4*a+qq
            tot=None
            for j in range(7):
                v=acc[pl.ds(32*j,32),128*kr:128*kr+128]
                sh=(32*qq-16*j)%128
                if sh: v=pltpu.roll(v,sh,1)
                tot=v if tot is None else tot+v
            out=out+jnp.where(lane==qq,tot,0.0)
        sp[pl.ds(base+32*a,32),:]=out


def to_fixed(v):
    top = jnp.maximum(jnp.max(jnp.abs(v), 0, keepdims=True), 1e-30)
    e = jnp.ceil(jnp.log(top) * 1.4426950408889634)
    code = jnp.clip(jnp.round(v * jnp.exp((15.0 - e) * 0.6931471805599453)), -32767.0, 32767.0)
    return code.astype(jnp.int32).astype(jnp.int16), jnp.broadcast_to(e, (16, 128)).astype(jnp.int32).astype(jnp.int16)

def from_fixed(code, e):
    scale = jnp.exp((e.astype(jnp.int32).astype(F32)[0:1] - 15.0) * 0.6931471805599453)
    return code.astype(jnp.int32).astype(F32) * scale


def expand_bias(raw, stage, pack, bias):
    c1, c2, c3, dense, value, advantage = raw
    stage[...] = jnp.zeros_like(stage)
    stage[0:1, 0:32] = c1[...].astype(F32)
    stage[1:2, 0:64] = c2[...].astype(F32)
    stage[2:3, 0:64] = c3[...].astype(F32)
    stage[3:7, 0:128] = dense[...].astype(F32)
    stage[7:8, 0:ACTIONS] = advantage[...].astype(F32)
    heads = jnp.where(iota((1, 128), 1) == ACTIONS, value[...].astype(F32), stage[7:8, 0:128])
    stage[7:8, 0:128] = heads
    pack[...] = stage[0:8, 0:128].astype(BF)

    def tiled(width):
        e = (iota((128, 256), 1) % width == iota((128, 256), 0)).astype(F32).astype(BF)
        return dot(pack[...], e)
    lane = iota((1, 256), 1)
    zero = jnp.zeros((1, 256), F32)
    t32, t64 = tiled(32), tiled(64)
    bias[:, 0:256] = jnp.where(lane < 224, t32[0:1], zero)
    bias[:, 256:512] = t64[1:2]
    bias[:, 512:768] = t64[1:2]
    bias[:, 768:896] = jnp.where(lane < 64, t64[1:2], zero)[:, 0:128]
    bias[:, 896:1152] = t64[2:3]
    bias[:, 1152:1408] = jnp.where(lane < 192, t64[2:3], zero)
    wide = pack[...].astype(F32)
    for k in range(5):
        bias[:, 1408 + 128 * k:1536 + 128 * k] = wide[3 + k:4 + k]


def prepare_heads(value, advantage, legal, stage, head_w, legal_t):
    stage[...] = jnp.zeros_like(stage)
    stage[0:ACTIONS, :] = advantage[...].astype(F32)
    stage[ACTIONS:ACTIONS + 1, :] = value[...].astype(F32)
    head_w[...] = stage[...].astype(BF)
    stage[...] = jnp.zeros_like(stage)
    stage[0:ACTIONS, 0:legal.shape[1]] = legal[...].astype(F32)
    row = iota((128, 128), 0)
    legal_t[...] = jnp.where(row == 0, 1.0, stage[:, 0:128]).astype(BF)


def prepare_meta(act, game, ret, boot, weight, index, count, stage, meta_out):
    cap, peers = act.shape
    stage[:, 0:128] = jnp.zeros((128, 128), F32)
    fields = (
        act[...].astype(F32),
        game[...].astype(F32),
        ret[...] + GAMMA_THREE * boot[...],
        weight[...],
        index[...].astype(F32),
        (iota((cap, peers), 0) < count[...]).astype(F32),
    )
    for k, field in enumerate(fields):
        stage[8 * k:8 * k + cap, 0:peers] = field
    by_peer = stage[:, 0:128].T
    rows = 8 * peers
    repeat = (iota((rows, 128), 1) == iota((rows, 128), 0) // 8).astype(F32).astype(BF)
    spread = sum(dot(repeat, part) for part in split3(by_peer))
    spread = jnp.where(iota((rows, 128), 0) % 8 == iota((rows, 128), 1) % 8, spread, 0.0)
    collect = (iota((128, 128), 0) // 8 == iota((128, 128), 1)).astype(F32).astype(BF)
    meta_out[...] = sum(dot(part, collect) for part in split3(spread))


def learner_kernel(
    sizes,
    x_in, act, game, ret, boot, weight, index, count, table, legal, w1, w2, w3, r1, r2, r3, r4, rv, ra, value, advantage,
    dense_in,
    dg_out, sp_out, lp_out, q_out, tab_out,
    x_buf, x3, a1, s1, a2, s2, a3, s3, g3, g2, dw, t1, t2a, t2b, t2c, t3a, t3b, u2, u3, acc,
    bias, stage, pack, head_w, legal_t, meta_out, meta_in, q_send, q_in, a3t, a_in, g4_send, g4_in,
    part, codes, z_in, dg, sp, sp_in, sp_mid, sp_z, sp_all, lp, lp_in, lp_mid, lp_z, lp_all,
    x_sem, dw_sem, out_sem, leave_sem, join_sem, act_sem, act_core_sem, z_sem, near_sem, diag_sem,
):
    hsize, dsize, zrows = sizes
    zsize = dsize // 2
    peers = hsize * dsize
    region = sum(zrows) * (zsize // 2)
    group, share = small_group(sizes)
    h = lax.axis_index("hst")
    d = lax.axis_index("dev")
    z = d // 2
    core = d % 2
    mine = 2 * h + core
    me = h * dsize + d

    def where_is(peer):
        return (peer // dsize, peer % dsize)

    arrive = {
        "act": act_sem, "act_core": act_core_sem, "gather_z": z_sem, "gather_near": near_sem, "gather_diag": diag_sem,
    }

    def transfer(kind, at, src, dst, device):
        leave = leave_sem.at[LEAVE.index(kind if kind in LEAVE else kind + str(at[0]))]
        if kind in arrive:
            join = arrive[kind].at[at]
        else:
            join = join_sem.at[JOIN.index(kind if kind in JOIN else kind + str(at[0]))]
        return pltpu.make_async_remote_copy(
            src_ref=src, dst_ref=dst, send_sem=leave, recv_sem=join, device_id=device, device_id_type=MESH
        )

    def send(kind, at, src, dst, device):
        transfer(kind, at, src, dst, device).start()

    def landed(kind, at, dst):
        transfer(kind, at, dst, dst, (h, d)).wait_recv()

    def sent(kind, at, src):
        transfer(kind, at, src, src, (h, d)).wait_send()

    def fetch(c, slot, count=PIXELS):
        return pltpu.make_async_copy(
            x_in.at[pl.ds(pl.multiple_of(PIXELS * c, 16), count)], x_buf.at[slot, pl.ds(0, count)], x_sem.at[slot]
        )

    last = h >= 0

    @pl.when(last)
    def _():
        for c in range(SLOTS):
            fetch(c, c).start()
        barrier = pltpu.get_barrier_semaphore()

        def greet(k, carry):
            pl.semaphore_signal(barrier, inc=1, device_id=where_is((me + k) % peers), device_id_type=MESH)
            return carry

        lax.fori_loop(1, peers, greet, 0)
        pltpu.make_async_copy(dense_in, dw.at[pl.ds(0, FLAT)], dw_sem).start()
        dw[pl.ds(FLAT, 64)] = jnp.zeros((64, HIDDEN), BF)
        build_toeplitz(w1, w2, w3, t1, t2a, t2b, t2c, t3a, t3b)

    @pl.when(last)
    def _():
        expand_bias((r1, r2, r3, r4, rv, ra), stage, pack, bias)
        prepare_heads(value, advantage, legal, stage, head_w, legal_t)
        prepare_meta(act, game, ret, boot, weight, index, count, stage, meta_out)

    def chunk(c, carry):
        slot = c % SLOTS
        fetch(c, slot).wait()
        relayout(x_buf.at[slot], x3, 8 * c + 4)

        conv1_rows(c, x3, t1, bias, a1, s1)

        @pl.when(c + SLOTS < CHUNKS - 1)
        def _():
            fetch(c + SLOTS, slot).start()

        @pl.when(c + SLOTS == CHUNKS - 1)
        def _():
            fetch(CHUNKS - 1, slot, PIXELS // 2).start()

        return carry

    lax.fori_loop(0, 4, chunk, 0)

    @pl.when(last)
    def _():
        pl.semaphore_wait(pltpu.get_barrier_semaphore(), peers - 1)

        def give(k, carry):
            peer = (me + k) % peers
            send(
                "meta", k, meta_out.at[pl.ds(pl.multiple_of(8 * peer, 8), 8)],
                meta_in.at[pl.ds(pl.multiple_of(8 * me, 8), 8)], where_is(peer),
            )
            return carry

        lax.fori_loop(1, peers, give, 0)

    lax.fori_loop(4, CHUNKS - 1, chunk, 0)

    @pl.when(last)
    def _():
        slot = (CHUNKS - 1) % SLOTS
        fetch(CHUNKS - 1, slot, PIXELS // 2).wait()
        relayout(x_buf.at[slot], x3, 8 * (CHUNKS - 1) + 4, 4)
        conv1_rows(CHUNKS - 1, x3, t1, bias, a1, s1, (0,))

    sibling = (h, 2 * z + 1 - core)
    row_me = pl.ds(pl.multiple_of(8 * me, 8), 8)
    hy, hx = h // 2, h % 2
    flip_x, flip_y = 2 * hy + 1 - hx, 2 * (1 - hy) + hx
    near = (1 - core) * flip_x + core * flip_y
    far = (1 - core) * flip_y + core * flip_x
    across = 3 - h

    def plane(j):
        return (j // 2, 2 * z + j % 2)

    def features(f, to):
        return a3t.at[pl.ds(pl.multiple_of(784 * to + START[f], 16), ROWS[f])]

    def received(f, src):
        return a_in.at[src, pl.ds(ROWS[0] * f, ROWS[f])]

    def send_features(f):
        for k in range(1, hsize):
            to = (h + k) % hsize
            send("act", (f, k), features(f, to), received(f, mine), (to, d))
        send("act_core", (f, 0), features(f, h), received(f, mine), sibling)

    def forward_features(f):
        for k in range(1, hsize):
            src = 2 * ((h - k + hsize) % hsize) + core
            landed("act", (f, k), received(f, src))
            send("act_core", (f, k), received(f, src), received(f, src), sibling)

    def partial(f):
        for k in range(hsize):
            src = 2 * ((h - k + hsize) % hsize) + 1 - core
            landed("act_core", (f, k), received(f, src))
        if f == 0:
            landed("g4", 0, g4_in.at[pl.ds(0, 2 * hsize - 1)])
        left = jnp.concatenate([received(f, j)[...] for j in range(2 * hsize)], 1)
        right = jnp.concatenate([g4_in[j] for j in range(2 * hsize)], 0)
        product = dot(left, right)
        n = zrows[f]
        spare = jnp.zeros((n * (zsize // 2) - ROWS[f], 128), F32)
        for lanes in range(2):
            column = product[:, 128 * lanes:128 * lanes + 128]
            if spare.shape[0]:
                column = jnp.concatenate([column, spare], 0)
            for j in range(zsize // 2):
                chunk = column[n * j:n * j + n]
                part[f, 2 * j + lanes, 0:n] = chunk
                codes[f, 2 * j + lanes, 0:n], codes[f, 2 * j + lanes, n:n + 16] = to_fixed(chunk)
        for k in range(1, zsize):
            to = (z + k) % zsize
            send("sum", (f, k), codes.at[f, to, pl.ds(0, n + 16)], z_in.at[f, z, pl.ds(0, n + 16)], (h, 2 * to + core))

    def corner(f, hh, zz, cc):
        rows = region * hh + zrows[0] * (zsize // 2) * f + zrows[f] * (zz // 2)
        return pl.multiple_of(rows, 16), pl.multiple_of(256 * cc + 128 * (zz % 2), 128)

    def place(f, hh, zz, cc):
        rows, lanes = corner(f, hh, zz, cc)
        return dg.at[pl.ds(rows, zrows[f]), pl.ds(lanes, 128)]

    def spread(f, zz, k):
        at = place(f, h, zz, core)
        send("gather_near", (f, 0, k), at, at, (near, d))
        send("gather_near", (f, 1, k), at, at, (far, d))
        send("gather_core", (f, 0, k), at, at, sibling)

    def finish(f):
        n = zrows[f]
        landed("sum", (f, 0), z_in.at[f, pl.ds(0, zsize - 1), pl.ds(0, n + 16)])
        total = part[f, z, 0:n]
        for k in range(1, zsize):
            src = (z - k + zsize) % zsize
            total = total + from_fixed(z_in[f, src, 0:n], z_in[f, src, n:n + 16])
        rows, lanes = corner(f, h, z, core)
        dg[pl.ds(rows, n), pl.ds(lanes, 128)] = total.astype(BF)
        at = place(f, h, z, core)
        for k in range(1, zsize):
            send("gather_z", (f, k), at, at, (h, 2 * ((z + k) % zsize) + core))
        spread(f, z, 0)

    def pass_on(f):
        for k in range(1, zsize):
            zz = (z - k + zsize) % zsize
            landed("gather_z", (f, k), place(f, h, zz, core))
            spread(f, zz, k)

    def pass_across(f, first=0, count=99):
        for k in range(first, min(first + count, zsize)):
            zz = (z - k + zsize) % zsize
            at = place(f, near, zz, core)
            landed("gather_near", (f, 0, k), at)
            send("gather_diag", (f, k), at, at, (far, d))
            send("gather_core", (f, 1, k), at, at, sibling)
            at = place(f, far, zz, core)
            landed("gather_near", (f, 1, k), at)
            send("gather_core", (f, 2, k), at, at, sibling)

    def pass_last(f):
        for k in range(zsize):
            at = place(f, across, (z - k + zsize) % zsize, core)
            landed("gather_diag", (f, k), at)
            send("gather_core", (f, 3, k), at, at, sibling)

    def gather_core(f):
        landed("gather_core", (f, 0), dg.at[pl.ds(0, zrows[f] * zsize)])

    def group_rows(j):
        return pl.ds(pl.multiple_of(group * j, 8), group)

    def share_rows(j, zz):
        return pl.ds(pl.multiple_of(group * j + share * zz, 8), share)

    def small_send():
        for k in range(1, 2 * hsize):
            to = (mine + k) % (2 * hsize)
            send("small", k, sp.at[group_rows(to)], sp_in.at[mine], plane(to))
        sp_in[mine] = sp[group_rows(mine), :]

    def small_sum():
        landed("small", 0, sp_in.at[pl.ds(0, 2 * hsize - 1)])
        total = sp_in[0]
        for j in range(1, 2 * hsize):
            total = total + sp_in[j]
        sp_mid[...] = total
        for k in range(1, zsize):
            to = (z + k) % zsize
            send("small_z", k, sp_mid.at[pl.ds(pl.multiple_of(share * to, 8), share)], sp_z.at[z], (h, 2 * to + core))
        sp_z[z] = sp_mid[pl.ds(pl.multiple_of(share * z, 8), share), :]

    def small_finish():
        landed("small_z", 0, sp_z.at[pl.ds(0, zsize - 1)])
        total = sp_z[0]
        for j in range(1, zsize):
            total = total + sp_z[j]
        sp_all[share_rows(mine, z), :] = total
        at = sp_all.at[share_rows(mine, z)]
        for k in range(1, zsize):
            send("small_back", k, at, at, (h, 2 * ((z + k) % zsize) + core))

    def small_spread():
        landed("small_back", 0, sp_z.at[pl.ds(0, zsize - 1)])
        at = sp_all.at[group_rows(mine)]
        for k in range(1, hsize):
            send("small_all", k, at, at, ((h + k) % hsize, d))
        send("small_core", 0, at, at, sibling)

    def small_share():
        landed("small_all", 0, sp_in.at[pl.ds(0, hsize - 1)])
        for k in range(1, hsize):
            at = sp_all.at[group_rows(2 * ((h - k + hsize) % hsize) + core)]
            send("small_core", k, at, at, sibling)

    def late_rows(j):
        return pl.ds(pl.multiple_of(16 * j, 16), 16)

    def late_send():
        for k in range(1, 2 * hsize):
            to = (mine + k) % (2 * hsize)
            send("late", k, lp.at[late_rows(to)], lp_in.at[mine], plane(to))
        lp_in[mine] = lp[late_rows(mine), :]

    def late_sum():
        landed("late", 0, lp_in.at[pl.ds(0, 2 * hsize - 1)])
        total = lp_in[0]
        for j in range(1, 2 * hsize):
            total = total + lp_in[j]
        lp_mid[...] = total
        lp_z[z] = total
        for k in range(1, zsize):
            send("late_z", k, lp_mid, lp_z.at[z], (h, 2 * ((z + k) % zsize) + core))

    def late_spread():
        landed("late_z", 0, lp_z.at[pl.ds(0, zsize - 1)])
        total = lp_z[0]
        for j in range(1, zsize):
            total = total + lp_z[j]
        lp_all[late_rows(mine), :] = total
        at = lp_all.at[late_rows(mine)]
        for k in range(1, 2 * hsize):
            send("late_all", k, at, at, plane((mine + k) % (2 * hsize)))

    def dense_out(f, cc, at):
        first, count = zrows[0] * (zsize // 2) * f, zrows[f] * (zsize // 2)
        lanes = pl.ds(pl.multiple_of(256 * cc, 128), 256)
        return [
            pltpu.make_async_copy(
                dg.at[pl.ds(region * j + first, count), lanes], dg_out.at[pl.ds(region * j + first, count), lanes],
                out_sem.at[hsize * (2 * f + at) + j],
            )
            for j in range(hsize)
        ]

    @pl.when(last)
    def _():
        conv2_all(a1, t2a, t2b, t2c, bias, a2, s2)
        conv3_all(a2, t3a, t3b, bias, a3, s3)
        for r in range(7):
            a3t[pl.ds(448 * r, 448), :] = a3[r].T[0:448]
        send_features(0)

    @pl.when(last)
    def _():
        pltpu.make_async_copy(dense_in, dw.at[pl.ds(0, FLAT)], dw_sem).wait()
        act4, slope4, head = dense_head(a3, dw, head_w, bias)

        landed("meta", 0, meta_in.at[pl.ds(0, 8 * (peers - 1))])
        meta_in[row_me, :] = meta_out[row_me, :]
        q, grow, dhb, loss, newt, top = td_part(
            head, meta_in[...], meta_out[...], legal_t[...], table[...], 8 * peers, float(peers * act.shape[0])
        )
        g4, dhw = head_grads(grow, act4, slope4, head_w)
        for half in range(2):
            g4_send[half] = g4[:, 256 * half:256 * half + 256]
        for k in range(1, 2 * hsize):
            to = (mine + k) % (2 * hsize)
            send("g4", k, g4_send.at[to % 2], g4_in.at[mine], plane(to))
        send_features(1)
        g4_in[mine] = g4_send[core]
        for f in range(2):
            received(f, mine)[...] = features(f, h)[...]
        tab_out[...] = jnp.broadcast_to(newt, (8, 128))
        lane = iota((8 * peers, 128), 1)
        q_send[...] = jnp.where(lane == 19, top, jnp.where(lane == 20, loss, q))
        for k in range(4):
            sp[pl.ds(640 + 24 * k, 24), :] = dhw[0:24, 128 * k:128 * k + 128]
        b4 = jnp.sum(g4.astype(F32), 0, keepdims=True)
        for k in range(4):
            sp[738 + k:739 + k, :] = b4[:, 128 * k:128 * k + 128]
        sp[742:743, :] = dhb
        sp[743:2 * hsize * group, :] = jnp.zeros((2 * hsize * group - 743, 128), F32)
        lp[64:, :] = jnp.zeros((lp.shape[0] - 64, 128), F32)
        sp[737:738, :] = fold64(g3_all(g4, dw, s3, g3))

    @pl.when(last)
    def _():
        build_transposed(w2, w3, u2, u3)

    @pl.when(last)
    def _():
        sp[736:737, :] = fold64(conv3_dx(g3, u3, s2, g2))
        forward_features(0)

    @pl.when(last)
    def _():
        conv3_dw(a2, g3, sp, 256)

    @pl.when(last)
    def _():
        conv2_dw(a1, g2, sp, 0, 0, 4)

    @pl.when(last)
    def _():
        partial(0)
        small_send()

    @pl.when(last)
    def _():
        stage[0:1, 0:256] = conv2_dx(g2, u2, s1, a1, 0, 2)
        forward_features(1)

    @pl.when(last)
    def _():
        b1 = conv2_dx(g2, u2, s1, a1, 2, 4) + stage[0:1, 0:256]
        b1 = b1[:, 0:128] + b1[:, 128:256]
        b1 = b1 + pltpu.roll(b1, 64, 1)
        lp[64:65, :] = b1 + pltpu.roll(b1, 32, 1)

    @pl.when(last)
    def _():
        partial(1)

    @pl.when(last)
    def _():
        conv1_dw(x3, a1, acc, 0, 2)

    @pl.when(last)
    def _():
        small_sum()
        finish(0)

    @pl.when(last)
    def _():
        conv1_dw(x3, a1, acc, 2, 5)

    @pl.when(last)
    def _():
        conv1_fold(acc, lp, 0)
        late_send()
        small_finish()
        pass_on(0)
        finish(1)
        late_sum()
        small_spread()
        pass_across(0)
        pass_on(1)

        def answer(k, carry):
            peer = (me + k) % peers
            send(
                "q", k, q_send.at[pl.ds(pl.multiple_of(8 * peer, 8), 8)],
                q_in.at[pl.ds(pl.multiple_of(8 * me, 8), 8)], where_is(peer),
            )
            return carry

        lax.fori_loop(1, peers, answer, 0)
        q_in[row_me, :] = q_send[row_me, :]

        pass_last(0)
        pass_across(1, 0, 2)
        late_spread()
        gather_core(0)
        first_half = dense_out(0, core, 0) + dense_out(0, 1 - core, 1)
        for copy in first_half:
            copy.start()
        pass_across(1, 2, zsize)
        small_share()
        pass_last(1)
        landed("small_core", 0, sp_in.at[pl.ds(0, hsize)])
        landed("late_all", 0, lp_in.at[pl.ds(0, 2 * hsize - 1)])

        landed("q", 0, q_in.at[pl.ds(0, 8 * (peers - 1))])
        others = [
            pltpu.make_async_copy(src, dst, out_sem.at[4 * hsize + k])
            for k, (src, dst) in enumerate(((sp_all, sp_out), (lp_all, lp_out), (q_in, q_out)))
        ]
        for copy in others:
            copy.start()
        own_half = dense_out(1, core, 0)
        for copy in own_half:
            copy.start()
        gather_core(1)
        other_half = dense_out(1, 1 - core, 1)
        for copy in other_half:
            copy.start()

        sent("meta", 0, meta_in.at[pl.ds(0, 8 * (peers - 1))])
        sent("q", 0, q_in.at[pl.ds(0, 8 * (peers - 1))])
        sent("act", (0, 0), a_in.at[pl.ds(0, hsize - 1)])
        sent("act_core", (0, 0), a_in.at[pl.ds(0, hsize)])
        sent("g4", 0, g4_in.at[pl.ds(0, 2 * hsize - 1)])
        sent("small", 0, sp_in.at[pl.ds(0, 2 * hsize - 1)])
        sent("small_z", 0, sp_z.at[pl.ds(0, zsize - 1)])
        sent("small_back", 0, sp_z.at[pl.ds(0, zsize - 1)])
        sent("small_all", 0, sp_in.at[pl.ds(0, hsize - 1)])
        sent("small_core", 0, sp_in.at[pl.ds(0, hsize)])
        sent("late", 0, lp_in.at[pl.ds(0, 2 * hsize - 1)])
        sent("late_z", 0, lp_z.at[pl.ds(0, zsize - 1)])
        sent("late_all", 0, lp_in.at[pl.ds(0, 2 * hsize - 1)])
        for f in range(2):
            n = zrows[f]
            sent("sum", (f, 0), z_in.at[f, pl.ds(0, zsize - 1), pl.ds(0, n + 16)])
            sent("gather_z", (f, 0), dg.at[pl.ds(0, n * (zsize - 1)), pl.ds(0, 128)])
            sent("gather_near", (f, 0, 0), dg.at[pl.ds(0, n * zsize), pl.ds(0, 256)])
            sent("gather_diag", (f, 0), dg.at[pl.ds(0, n * zsize), pl.ds(0, 128)])
            sent("gather_core", (f, 0), dg.at[pl.ds(0, n * zsize)])
        for copy in first_half + others + own_half + other_half:
            copy.wait()


def small_group(sizes):
    hsize, dsize, _ = sizes
    zsize = dsize // 2
    group = -(-743 // (2 * hsize * 8 * zsize)) * 8 * zsize
    return group, group // zsize


def learner(sizes, args, cap):
    hsize, dsize, zrows = sizes
    zsize, peers = dsize // 2, hsize * dsize
    region = sum(zrows) * (zsize // 2)
    group, share = small_group(sizes)
    dma = pltpu.SemaphoreType.DMA
    vmem = pltpu.VMEM
    groups = 2 * hsize
    scratch = [
        vmem((SLOTS, PIXELS, 128), BF), vmem((88, 128, 384), BF), vmem((21, 128, 768), BF), vmem((21, 128, 768), F32), vmem((9, 128, 640), BF),
        vmem((9, 128, 640), F32), vmem((7, 128, 512), BF), vmem((7, 128, 512), F32), vmem((11, 128, 512), BF),
        vmem((11, 128, 640), BF), vmem((3200, 512), BF), vmem((1024, 256), BF), vmem((2048, 256), BF),
        vmem((2048, 256), BF), vmem((1024, 128), BF), vmem((1536, 256), BF), vmem((1152, 256), BF),
        vmem((2, 2304, 256), BF), vmem((3072, 256), BF), vmem((256, 1024), F32),
        vmem((1, 2048), F32), vmem((128, 512), F32), vmem((8, 128), BF), vmem((128, 512), BF), vmem((128, 128), BF),
        vmem((8 * peers, 128), F32), vmem((8 * peers, 128), F32), vmem((8 * peers, 128), F32),
        vmem((8 * peers, 128), F32), vmem((FLAT, 128), BF), vmem((groups, sum(ROWS), 128), BF), vmem((2, 128, 256), BF),
        vmem((groups, 128, 256), BF), vmem((2, zsize, max(zrows), 128), F32), vmem((2, zsize, max(zrows) + 16, 128), jnp.int16),
        vmem((2, zsize, max(zrows) + 16, 128), jnp.int16), vmem((hsize * region, 512), BF),
        vmem((groups * group, 128), F32), vmem((groups, group, 128), F32), vmem((group, 128), F32),
        vmem((zsize, share, 128), F32), vmem((groups * group, 128), F32),
        vmem((16 * groups, 128), F32), vmem((groups, 16, 128), F32), vmem((16, 128), F32), vmem((zsize, 16, 128), F32),
        vmem((16 * groups, 128), F32),
        dma((SLOTS,)), dma, dma((4 * hsize + 3,)), dma((len(LEAVE),)), dma((len(JOIN),)),
        dma((2, hsize)), dma((2, hsize)), dma((2, zsize)), dma((2, 2, zsize)), dma((2, zsize)),
    ]
    whole = pl.BlockSpec(memory_space=pltpu.VMEM)
    outside = pl.BlockSpec(memory_space=pl.ANY)
    return pl.pallas_call(
        functools.partial(learner_kernel, sizes),
        in_specs=[outside] + [whole] * 20 + [outside],
        out_specs=[outside, outside, outside, outside, whole],
        out_shape=[
            jax.ShapeDtypeStruct((hsize * region, 512), BF),
            jax.ShapeDtypeStruct((groups * group, 128), F32),
            jax.ShapeDtypeStruct((16 * groups, 128), F32),
            jax.ShapeDtypeStruct((8 * peers, 128), F32),
            jax.ShapeDtypeStruct((8, 128), F32),
        ],
        scratch_shapes=scratch,
        compiler_params=pltpu.CompilerParams(collective_id=0, has_side_effects=True, vmem_limit_bytes=63 << 20),
    )(*args)


def output_kernel(
    hsize, region, second, dg, sp, lp, q, tab,
    dense, c1, c2, c3, bias1, bias2, bias3, bias4, vw, vb, aw, ab, loss, top, table, qt,
    held, wide, in_sem, out_sem,
):
    reads = []
    for j in range(2 * hsize):
        f = j % 2
        src, at, count = region * (j // 2) + f * (second + 16), 784 * (j // 2) + f * ROWS[0], ROWS[f] - 16 * f
        copy = pltpu.make_async_copy(dg.at[pl.ds(src, count)], held.at[pl.ds(at, count)], in_sem.at[j])
        reads.append((copy, at, count))
    for copy, _, _ in reads:
        copy.start()
    for a in range(2):
        c1[pl.ds(128 * a, 128), :] = lp[pl.ds(32 * a, 32), :].T
    for kr in range(4):
        c2[pl.ds(128 * kr, 128), :] = sp[pl.ds(64 * kr, 64), :].T
    for kr in range(3):
        c3[pl.ds(192 * kr, 128), :] = sp[pl.ds(256 + 128 * kr, 64), :].T
        c3[pl.ds(192 * kr + 128, 64), :] = sp[pl.ds(320 + 128 * kr, 64), :].T[0:64]
    bias1[...] = lp[64:65, 0:32]
    bias2[...] = sp[736:737, 0:64]
    bias3[...] = sp[737:738, 0:64]
    for k in range(4):
        bias4[:, 128 * k:128 * k + 128] = sp[738 + k:739 + k, :]
        heads = sp[pl.ds(640 + 24 * k, 24), :]
        aw[:, 128 * k:128 * k + 128] = heads[0:ACTIONS]
        vw[:, 128 * k:128 * k + 128] = heads[ACTIONS:ACTIONS + 1]
    ab[...] = sp[742:743, 0:ACTIONS]
    vb[...] = sp[742:743, ACTIONS:ACTIONS + 1]
    rows = q[...]
    top[...] = jnp.max(rows[:, 19:20], 0, keepdims=True)
    first = iota((rows.shape[0], 1), 0) % 8 == 0
    loss[...] = jnp.sum(jnp.where(first, rows[:, 20:21], 0.0), 0, keepdims=True)
    table[...] = tab[0:1, :]
    turned = rows.T
    for k in range(ACTIONS):
        qt[k] = turned[k:k + 1]
    writes = []
    for j, (copy, at, count) in enumerate(reads):
        copy.wait()
        wide[pl.ds(at, count)] = held[pl.ds(at, count)].astype(F32)
        writes.append(pltpu.make_async_copy(wide.at[pl.ds(at, count)], dense.at[pl.ds(at, count)], out_sem.at[j]))
        writes[-1].start()
    for copy in writes:
        copy.wait()


def outputs(sizes, dg, sp, lp, q, tab):
    hsize, dsize, zrows = sizes
    region, second = sum(zrows) * (dsize // 4), zrows[0] * (dsize // 4)
    whole = pl.BlockSpec(memory_space=pltpu.VMEM)
    outside = pl.BlockSpec(memory_space=pl.ANY)
    shapes = (
        (FLAT, 512), (256, 32), (512, 64), (576, 64), (1, 32), (1, 64), (1, 64), (1, 512), (1, 512), (1, 1),
        (ACTIONS, 512), (1, ACTIONS), (1, 1), (1, 1), (1, 128), (ACTIONS, 1, 8 * hsize * dsize),
    )
    return pl.pallas_call(
        functools.partial(output_kernel, hsize, region, second),
        in_specs=[outside, whole, whole, whole, whole],
        out_specs=[outside] + [whole] * 15,
        out_shape=[jax.ShapeDtypeStruct(s, F32) for s in shapes],
        scratch_shapes=[
            pltpu.VMEM((FLAT, 512), BF), pltpu.VMEM((FLAT, 512), F32),
            pltpu.SemaphoreType.DMA((2 * hsize,)), pltpu.SemaphoreType.DMA((2 * hsize,)),
        ],
        compiler_params=pltpu.CompilerParams(vmem_limit_bytes=63 << 20),
    )(dg, sp, lp, q, tab)


def per_device(
    hsize,
    dsize,
    replay,
    send_index,
    send_count,
    actions,
    game_ids,
    legal_table,
    returns,
    bootstrap,
    is_weights,
    priority_table,
    conv1_w,
    conv1_b,
    conv2_w,
    conv2_b,
    conv3_w,
    conv3_b,
    dense_w,
    dense_b,
    value_w,
    value_b,
    advantage_w,
    advantage_b,
):
    cap = send_index.shape[2]
    peers = hsize * dsize
    zsize = dsize // 2
    zrows = tuple(-(-rows // (8 * zsize)) * 16 for rows in ROWS)
    sizes = (hsize, dsize, zrows)
    args = (
        replay.T,
        actions[0].T,
        game_ids[0].T,
        returns[0].T,
        bootstrap[0].T,
        is_weights[0].T,
        send_index[0].T,
        send_count,
        priority_table.reshape(1, -1),
        legal_table.T,
        conv1_w.reshape(256, 32),
        conv2_w.reshape(512, 64),
        conv3_w.reshape(576, 64),
        conv1_b.reshape(1, -1),
        conv2_b.reshape(1, -1),
        conv3_b.reshape(1, -1),
        dense_b.reshape(4, -1),
        value_b.reshape(1, -1),
        advantage_b.reshape(1, -1),
        value_w.T,
        advantage_w.T,
        dense_w,
    )
    dg, sp, lp, q, tab = learner(sizes, args, cap)
    (dense, c1, c2, c3, b1, b2, b3, b4, vw, vb, aw, ab, loss, top, table, qt) = outputs(sizes, dg, sp, lp, q, tab)
    q_values = qt.transpose(1, 2, 0)
    if cap != 8:
        q_values = q_values.reshape(1, peers, 8, ACTIONS)[:, :, :cap].reshape(1, peers * cap, ACTIONS)
    return (
        q_values,
        loss.reshape(()),
        c1.reshape(conv1_w.shape),
        b1.reshape(-1),
        c2.reshape(conv2_w.shape),
        b2.reshape(-1),
        c3.reshape(conv3_w.shape),
        b3.reshape(-1),
        dense,
        b4.reshape(-1),
        vw.T,
        vb.reshape(-1),
        aw.T,
        ab.reshape(-1),
        table.reshape(-1),
        top.reshape(()),
    )


def solution(mesh):
    both = ("hst", "dev")
    rows2, rows3 = P(both, None), P(both, None, None)
    placed = (rows2, rows3, rows2, rows3, rows3, P(), rows3, rows3, rows3, P(both)) + (P(),) * 12
    return jax.shard_map(
        functools.partial(per_device, mesh.shape["hst"], mesh.shape["dev"]),
        mesh=mesh,
        in_specs=placed,
        out_specs=(rows3,) + (P(),) * 13 + (P(both), P()),
        check_vma=False,
    )
```
